32 devices in a mesh: rep: 2 (over x), region: 16 (over z, y, core).
Axes of the slice: x: 2, y: 2, z: 4, core: 2. Of those that a mesh axis runs over, the one named last changes fastest.
Arguments:
- nodes: bfloat16 [8192, 512], P(('rep', 'region')), parts along dimension 0, may hold values from -6 to 6
- edges: bfloat16 [65536, 512], P(('rep', 'region')), parts along dimension 0, may hold values from -6 to 6
- edge_cot: bfloat16 [65536, 512], P(('rep', 'region')), parts along dimension 0, may hold values from -6 to 6
- agg_cot: bfloat16 [8192, 512], P(('rep', 'region')), parts along dimension 0, may hold values from -6 to 6
- w_in: bfloat16 [1536, 512], replicated, may hold values from -0.15625 to 0.15625
- b_in: float32 [512], replicated, may hold values from -4 to 4
- w_out: bfloat16 [512, 512], replicated, may hold values from -0.25 to 0.25
- b_out: float32 [512], replicated, may hold values from -4 to 4
- gain: float32 [512], replicated, may hold values from 0.1 to 1.9
- send_rows: int32 [256, 16], P('region'), may hold values from 0 to 255, as said below
- edge_slot: int32 [32768], P('region'), may hold values from 0 to 255, as said below
- edge_receiver: int32 [32768], P('region'), may hold values from 0 to 255
- edge_count: int32 [16], P('region'), may hold values from 128 to 2048, as said below
Outputs:
- grad_edges: bfloat16 [65536, 512], P(('rep', 'region')), parts along dimension 0
- grad_nodes: float32 [8192, 512], P(('rep', 'region')), parts along dimension 0
- grad_w_in: bfloat16 [3072, 512], P('rep'), parts along dimension 0
- grad_w_out: bfloat16 [1024, 512], P('rep'), parts along dimension 0
- grad_vectors: bfloat16 [6, 512], P('rep'), parts along dimension 0
The draws below stay inside these ranges and needn't reach their ends.
There are 2 independent parts, one for each index of `rep`. The reference program is written for one: setup_inputs(seed, part) draws one part's arguments, and reference() takes and returns one part's arrays. A program takes and returns all parts, laid end to end along the dimension named above; an argument that names none is the same for every part. Nothing has to cross between parts.
Inputs may be any that keep to these rules, and one draw needn't show every extreme that they name: `send_rows`: row p * 16 + q lists, in its first slots, the local rows of region p's nodes that region q's edges read as senders; the remaining slots hold 0 and no edge reads them. Region q uses all 16 slots from itself and from its two neighbours p = q - 1 and q + 1 (modulo 16), and at least 4 slots from every region. With s = edge_slot[e] for an edge of region q, s // 16 is the region that sends the row and s % 16 a used slot of row (s // 16) * 16 + q of send_rows. Edges at local positions edge_count[q] and above in region q are padding; every count is a multiple of 128, and in every draw one region holds 2048 real edges.
All inputs are finite; a program needn't handle non-finite values.
Results may differ from the reference program's by a relative error of at most 0.0055.
Values may be sent and summed in bfloat16 or wider, within the bound.
No kernel may reach another device: no remote copies, remote signals or barrier semaphores. Data moves between devices by JAX's collectives and lax.ppermute only.
A program may use at most 128 MiB of HBM per device.

```python
import math
import jax
import jax.numpy as jnp
from jax import lax

D = 512
NODE_DEV = 256
EDGE_DEV = 2048
CAP = 16
NODES = 4096
EDGES = 32768
N_REGION = 16


def link_counts(key):
    low_counts = jax.random.randint(key, (N_REGION, N_REGION), max(1, CAP // 4), CAP + 1)
    source = jnp.arange(N_REGION)[:, None]
    target = jnp.arange(N_REGION)[None, :]
    cycle_gap = jnp.abs(source - target)
    cycle_gap = jnp.minimum(cycle_gap, N_REGION - cycle_gap)
    return jnp.where(cycle_gap <= 1, CAP, low_counts).astype(jnp.int32)


def draw_send_rows(key, part):
    slot_count = link_counts(key)
    key = jax.random.fold_in(key, 3)
    row_ids = jax.random.randint(key, (N_REGION * N_REGION, CAP), 0, NODE_DEV)
    used_slots = jnp.arange(CAP)[None, :] < slot_count.reshape(-1, 1)
    return jnp.where(used_slots, row_ids, 0).astype(jnp.int32)


def draw_edge_slot(key, part):
    slot_count = link_counts(key)
    key = jax.random.fold_in(key, 5)
    key_near, key_far, key_choose, key_offset = jax.random.split(key, 4)
    owner_dev = jnp.arange(EDGES) // EDGE_DEV
    near_step = jax.random.randint(key_near, (EDGES,), -1, 2)
    far_source = jax.random.randint(key_far, (EDGES,), 0, N_REGION)
    choose = jax.random.randint(key_choose, (EDGES,), 0, 4)
    source = jnp.where(choose < 3, (owner_dev + near_step + N_REGION) % N_REGION, far_source)
    used = slot_count[source, owner_dev]
    offset = jax.random.randint(key_offset, (EDGES,), 0, 1 << 20) % used
    return (source * CAP + offset).astype(jnp.int32)


def draw_edge_count(key, part):
    key = jax.random.fold_in(key, 7)
    key_base, key_full = jax.random.split(key)
    blocks = EDGE_DEV // 128
    base_count = jax.random.randint(key_base, (N_REGION,), max(1, blocks // 8), blocks // 2 + 1) * 128
    full_device = jax.random.randint(key_full, (), 0, N_REGION)
    return jnp.where(jnp.arange(N_REGION) == full_device, EDGE_DEV, base_count).astype(jnp.int32)


def with_ends(drawn, stream_key, least, top_value):
    spot = [jax.random.randint(jax.random.fold_in(stream_key, axis), (), 0, length) for axis, length in enumerate(drawn.shape)]
    main_axis = drawn.shape.index(max(drawn.shape))
    beside = spot[:main_axis] + [(spot[main_axis] + 1) % drawn.shape[main_axis]] + spot[main_axis + 1:]
    return drawn.at[tuple(spot)].set(least).at[tuple(beside)].set(top_value)


def levels(stream_key, extent, pieces, least, largest):
    def one(axis_at, blocks):
        steps = jax.random.uniform(jax.random.fold_in(jax.random.fold_in(stream_key, 6), axis_at), (blocks,), jnp.float32, least / len(pieces), largest / len(pieces))
        return jnp.repeat(jnp.exp(steps), extent[axis_at] // blocks).reshape((-1,) + (1,) * (len(extent) - axis_at - 1))

    level = one(*pieces[0])
    for cut in pieces[1:]:
        level = level * one(*cut)
    return level


def noise(stream_key, dims, width, most, shards=(), held_as=jnp.bfloat16):
    array = width * jax.random.normal(stream_key, dims, jnp.float32)
    if shards:
        array = array * levels(stream_key, dims, shards, -0.22, 0.18)
    return jnp.clip(array, -most, most).astype(held_as)


def setup_inputs(seed: int = 0, part: int = 0) -> dict:
    streams_of = jax.random.split(jax.random.key(seed), 14)
    part_splits = jax.random.split(jax.random.fold_in(streams_of[13], part), 14)
    return {
        "nodes": noise(part_splits[0], (NODES, D), 1.0, 6.0, ((0, 16),)),
        "edges": noise(part_splits[1], (EDGES, D), 1.0, 6.0, ((0, 16),)),
        "edge_cot": noise(part_splits[2], (EDGES, D), 1.0, 6.0, ((0, 16),)),
        "agg_cot": noise(part_splits[3], (NODES, D), 1.0, 6.0, ((0, 16),)),
        "w_in": noise(streams_of[4], (3 * D, D), (3 * D) ** -0.5, 0.15625),
        "b_in": noise(streams_of[5], (D,), 1.0, 4.0, (), jnp.float32),
        "w_out": noise(streams_of[6], (D, D), D ** -0.5, 0.25),
        "b_out": noise(streams_of[7], (D,), 1.0, 4.0, (), jnp.float32),
        "gain": jnp.clip(1.0 + 0.18 * jax.random.normal(streams_of[8], (D,), jnp.float32), 0.1, 1.9),
        "send_rows": draw_send_rows(jax.random.fold_in(streams_of[13], 71), part),
        "edge_slot": draw_edge_slot(jax.random.fold_in(streams_of[13], 71), part),
        "edge_receiver": with_ends(jax.random.randint(streams_of[11], (EDGES,), 0, NODE_DEV), jax.random.fold_in(streams_of[11], 1), 0, NODE_DEV - 1).astype(jnp.int32),
        "edge_count": draw_edge_count(jax.random.fold_in(streams_of[13], 71), part),
    }


def edge_backward(edges, senders, receivers, message_cot, w_in, b_in, w_out, b_out, gain):
    features = edges.shape[1]
    joined = jnp.concatenate([edges, senders, receivers], axis=1)
    pre_act = jnp.dot(joined, w_in, preferred_element_type=jnp.float32) + b_in
    activated = jax.nn.silu(pre_act).astype(jnp.bfloat16)
    pre_norm = jnp.dot(activated, w_out, preferred_element_type=jnp.float32) + b_out
    row_mean = lax.optimization_barrier(jnp.mean(pre_norm, axis=1, keepdims=True))
    centered = pre_norm - row_mean
    inv_std = lax.rsqrt(lax.optimization_barrier(jnp.mean(centered * centered, axis=1, keepdims=True)) + 1e-05)
    normed = centered * inv_std
    scaled = message_cot * gain
    d_norm = inv_std * (scaled - lax.optimization_barrier(jnp.mean(scaled, axis=1, keepdims=True)) - normed * lax.optimization_barrier(jnp.mean(scaled * normed, axis=1, keepdims=True)))
    d_norm_b = d_norm.astype(jnp.bfloat16)
    dw_out = lax.dot_general(activated, d_norm_b, (((0,), (0,)), ((), ())), preferred_element_type=jnp.float32)
    d_act = lax.dot_general(d_norm_b, w_out, (((1,), (1,)), ((), ())), preferred_element_type=jnp.float32)
    sigmoid_pre = jax.nn.sigmoid(pre_act)
    d_pre = d_act * sigmoid_pre * (1.0 + pre_act * (1.0 - sigmoid_pre))
    d_pre_b = d_pre.astype(jnp.bfloat16)
    dw_in = lax.dot_general(joined, d_pre_b, (((0,), (0,)), ((), ())), preferred_element_type=jnp.float32)
    d_joined = lax.dot_general(d_pre_b, w_in, (((1,), (1,)), ((), ())), preferred_element_type=jnp.float32)
    vectors = jnp.stack([lax.optimization_barrier(jnp.sum(d_pre, axis=0)), lax.optimization_barrier(jnp.sum(d_norm, axis=0)), lax.optimization_barrier(jnp.sum(message_cot * normed, axis=0))])
    grad_edge = (message_cot + d_joined[:, :features]).astype(jnp.bfloat16)
    return (grad_edge, d_joined[:, features:2 * features], d_joined[:, 2 * features:], dw_in, dw_out, vectors)

def reference(nodes, edges, edge_cot, agg_cot, w_in, b_in, w_out, b_out, gain, send_rows, edge_slot, edge_receiver, edge_count):
    owner_dev = (jnp.arange(EDGES) // EDGE_DEV).astype(jnp.int32)
    source = (edge_slot // CAP).astype(jnp.int32)
    local_row = send_rows[source * N_REGION + owner_dev, edge_slot % CAP]
    sender_ids = (source * NODE_DEV + local_row).astype(jnp.int32)
    receiver_ids = (owner_dev * NODE_DEV + edge_receiver).astype(jnp.int32)

    def device_block(totals, inputs):
        sum_in, sum_out, sum_vec, node_grads = totals
        blk_edges, blk_cot, blk_send, blk_recv, blk_count = inputs
        live_rows = (jnp.arange(EDGE_DEV) < blk_count).astype(jnp.float32)
        message_cot = (blk_cot.astype(jnp.float32) + agg_cot[blk_recv].astype(jnp.float32)) * live_rows[:, None]
        grad_edge, d_send, d_recv, dw_in, dw_out, vectors = edge_backward(blk_edges, nodes[blk_send], nodes[blk_recv], message_cot, w_in, b_in, w_out, b_out, gain)
        node_grads = node_grads.at[blk_send].add(d_send).at[blk_recv].add(d_recv)
        return ((sum_in + dw_in, sum_out + dw_out, sum_vec + vectors, node_grads), grad_edge)
    initial = (jnp.zeros((3 * D, D), jnp.float32), jnp.zeros((D, D), jnp.float32), jnp.zeros((3, D), jnp.float32), jnp.zeros((NODES, D), jnp.float32))
    scanned = (edges.reshape(N_REGION, EDGE_DEV, D), edge_cot.reshape(N_REGION, EDGE_DEV, D), sender_ids.reshape(N_REGION, EDGE_DEV), receiver_ids.reshape(N_REGION, EDGE_DEV), edge_count)
    (sum_in, sum_out, sum_vec, node_grads), grad_edges = lax.scan(device_block, initial, scanned)
    total_sq = jnp.sum(sum_in * sum_in) + jnp.sum(sum_out * sum_out) + jnp.sum(sum_vec * sum_vec)
    clip_limit = math.sqrt(4.0 * D * D + 3.0 * D)
    clip_scale = jnp.minimum(1.0, clip_limit / jnp.sqrt(total_sq + 1e-06))
    return (grad_edges.reshape(EDGES, D), node_grads, (sum_in * clip_scale).astype(jnp.bfloat16), (sum_out * clip_scale).astype(jnp.bfloat16), (sum_vec * clip_scale).astype(jnp.bfloat16))
```

```python
import functools
import math

import jax
import jax.numpy as jnp
from jax import lax
from jax.experimental import pallas as pl
from jax.experimental.pallas import tpu as pltpu
from jax.sharding import PartitionSpec as P

BF = jnp.bfloat16
F32 = jnp.float32
VMEM = pltpu.VMEM
SMEM = pltpu.SMEM
LIMIT = 60 * 1024 * 1024
SMALL = 16 * 1024 * 1024
EXTRA = 16


def dot(a, b, dims):
    return lax.dot_general(a, b, ((dims[0], dims[1]), ((), ())), preferred_element_type=F32)


NN = ((1,), (0,))
NT = ((1,), (1,))
TN = ((0,), (0,))


def one_hot_t(index_row, count):
    wide = lax.broadcasted_iota(jnp.int32, (count, index_row.shape[1]), 0) == index_row
    return jnp.where(wide, 1.0, 0.0).astype(BF)


def params(semantics=None):
    if semantics is None:
        return pltpu.CompilerParams(vmem_limit_bytes=LIMIT)
    return pltpu.CompilerParams(vmem_limit_bytes=LIMIT, dimension_semantics=semantics)


def whole(shape):
    return pl.BlockSpec(shape, lambda *i: (0,) * len(shape))


def cost(flops, nbytes):
    return pl.CostEstimate(flops=int(flops), bytes_accessed=int(nbytes), transcendentals=0)


def pick_kernel(index_ref, nodes_ref, out_ref):
    out_ref[...] = dot(one_hot_t(index_ref[...], nodes_ref.shape[0]), nodes_ref[...], TN).astype(BF)


def pick_rows(index_row, nodes):
    return pl.pallas_call(
        pick_kernel,
        out_shape=jax.ShapeDtypeStruct((index_row.shape[1], nodes.shape[1]), BF),
        compiler_params=params(),
    )(index_row, nodes)


def local_kernel(recv_ref, edges_ref, nodes_ref, w_e_ref, w_r_ref, b_ref, pre_ref, table):
    @pl.when(pl.program_id(0) == 0)
    def _():
        table[...] = dot(nodes_ref[...], w_r_ref[...], NN).astype(BF)

    got = dot(one_hot_t(recv_ref[...], nodes_ref.shape[0]), table[...], TN)
    pre_ref[...] = (dot(edges_ref[...], w_e_ref[...], NN) + got + b_ref[...]).astype(BF)


def local_part(recv_row, edges, nodes, w_in, b_row, block):
    total, f = edges.shape
    n = nodes.shape[0]
    edge_spec = pl.BlockSpec((block, f), lambda i: (i, 0))
    return pl.pallas_call(
        local_kernel,
        grid=(total // block,),
        in_specs=[
            pl.BlockSpec((1, block), lambda i: (0, i)),
            edge_spec,
            whole((n, f)),
            pl.BlockSpec((f, f), lambda i: (0, 0)),
            pl.BlockSpec((f, f), lambda i: (2, 0)),
            whole((1, f)),
        ],
        out_specs=edge_spec,
        out_shape=jax.ShapeDtypeStruct((total, f), BF),
        scratch_shapes=[VMEM((n, f), BF)],
        compiler_params=params(("arbitrary",)),
        cost_estimate=cost(2 * total * f * (f + n), 4 * total * f),
    )(recv_row, edges, nodes, w_in, w_in, b_row)


def slot_of(position, order):
    slot = 0
    for bit, mask in enumerate(reversed(order)):
        if position >> bit & 1:
            slot |= mask
    return slot


def write_slots(me, parts, keep_ref, send_ref, order, first=0):
    pieces = 2 ** len(order)
    home = me & (pieces - 1)
    r = parts[0].shape[0] // pieces
    for position in range(pieces):
        piece = home ^ slot_of(position, order)
        start = pl.multiple_of(piece * r, r)
        half, at = divmod(position, pieces // 2)
        ref = send_ref if half else keep_ref
        for k, acc in enumerate(parts):
            row = first + (at * len(parts) + k) * r
            ref[row : row + r, :] = acc[pl.ds(start, r), :].astype(ref.dtype)


def edge_kernel(order_p, order_q, blocks, me_ref, count_ref, slot_ref, recv_ref, edges_ref, cot_ref, pre_ref,
                nodes_ref, agg_ref, halo_ref, w_s_ref, w_out_ref, b_ref, gain_ref,
                dp_ref, keep_p, send_p, keep_q, send_q, sum_s_ref, sum_r_ref,
                table, acc_o, acc_e, acc_s, acc_r, acc_x, acc_y, sums):
    step = pl.program_id(0)
    rows, f = edges_ref.shape

    @pl.when(step == 0)
    def _():
        table[...] = dot(halo_ref[...], w_s_ref[...], NN).astype(BF)
        for ref in (acc_o, acc_e, acc_s, acc_r, sums):
            ref[...] = jnp.zeros_like(ref)

    hot_s = one_hot_t(slot_ref[...], halo_ref.shape[0])
    hot_r = one_hot_t(recv_ref[...], nodes_ref.shape[0])
    pre = pre_ref[...].astype(F32) + dot(hot_s, table[...], TN)
    sig = 0.5 * jnp.tanh(0.5 * pre) + 0.5
    silu = pre * sig
    act = silu.astype(BF)
    slope = sig + silu * (1.0 - sig)
    live = lax.broadcasted_iota(jnp.int32, (rows, f), 0) < count_ref[0] - step * rows
    mc = jnp.where(live, cot_ref[...].astype(F32) + dot(hot_r, agg_ref[...], TN), 0.0)
    norm_in = dot(act, w_out_ref[...], NN) + b_ref[...]
    inverse = 1.0 / f
    centered = norm_in - jnp.sum(norm_in, axis=1, keepdims=True) * inverse
    inv_std = lax.rsqrt(jnp.sum(centered * centered, axis=1, keepdims=True) * inverse + 1e-05)
    normed = centered * inv_std
    scaled = mc * gain_ref[...]
    mean_s = jnp.sum(scaled, axis=1, keepdims=True) * inverse
    mean_sn = jnp.sum(scaled * normed, axis=1, keepdims=True) * inverse
    dn = inv_std * (scaled - mean_s - normed * mean_sn)
    dn_b = dn.astype(BF)
    acc_o[...] += dot(act, dn_b, TN)
    sums[0:8, :] += jnp.sum(dn.reshape(rows // 8, 8, f), axis=0)
    sums[8:16, :] += jnp.sum((mc * normed).reshape(rows // 8, 8, f), axis=0)
    dp_b = (dot(dn_b, w_out_ref[...], NT) * slope).astype(BF)
    dp_ref[...] = dp_b
    acc_e[...] += dot(edges_ref[...], dp_b, TN)
    acc_s[...] += dot(hot_s, dp_b, NN)
    acc_r[...] += dot(hot_r, dp_b, NN)

    @pl.when(step == blocks - 1)
    def _():
        sum_s = acc_s[...].astype(BF)
        sum_r = acc_r[...].astype(BF)
        sum_s_ref[...] = sum_s
        sum_r_ref[...] = sum_r
        acc_x[...] = dot(halo_ref[...], sum_s, TN)
        acc_y[...] = dot(nodes_ref[...], sum_r, TN)
        me = me_ref[0]
        write_slots(me, (acc_x, acc_y), keep_p, send_p, order_p)
        write_slots(me, (acc_e, acc_o), keep_q, send_q, order_q, EXTRA)
        row = lax.broadcasted_iota(jnp.int32, (EXTRA // 2, f), 0)
        exact = jnp.where(row == 0, jnp.sum(acc_r[...], axis=0, keepdims=True), 0.0)
        exact = jnp.where(row == 1, jnp.sum(sums[0:8, :], axis=0, keepdims=True), exact)
        exact = jnp.where(row == 2, jnp.sum(sums[8:16, :], axis=0, keepdims=True), exact)
        high = exact.astype(BF).astype(F32)
        vectors = jnp.concatenate([high, exact - high], axis=0)
        keep_q[:EXTRA, :] = vectors
        send_q[:EXTRA, :] = vectors.astype(BF)


def edge_part(me, count, slot_row, recv_row, edges, edge_cot, pre, nodes, agg, halo, w_in, w_out, b_row, gain_row,
              order_p, order_q, block):
    total, f = edges.shape
    slots, n = halo.shape[0], nodes.shape[0]
    edge_spec = pl.BlockSpec((block, f), lambda i: (i, 0))
    index_spec = pl.BlockSpec((1, block), lambda i: (0, i))
    smem = pl.BlockSpec(memory_space=SMEM)
    shapes = [
        ((total, f), BF), ((f, f), F32), ((f, f), BF), ((f + EXTRA, f), F32), ((f + EXTRA, f), BF),
        ((slots, f), BF), ((n, f), BF),
    ]
    return pl.pallas_call(
        functools.partial(edge_kernel, order_p, order_q, total // block),
        grid=(total // block,),
        in_specs=[
            smem,
            smem,
            index_spec,
            index_spec,
            edge_spec,
            edge_spec,
            edge_spec,
            whole((n, f)),
            whole((n, f)),
            whole((slots, f)),
            pl.BlockSpec((f, f), lambda i: (1, 0)),
            whole((f, f)),
            whole((1, f)),
            whole((1, f)),
        ],
        out_specs=[edge_spec] + [whole(s) for s, _ in shapes[1:]],
        out_shape=[jax.ShapeDtypeStruct(s, d) for s, d in shapes],
        scratch_shapes=[
            VMEM((slots, f), BF), VMEM((f, f), F32), VMEM((f, f), F32), VMEM((slots, f), F32), VMEM((n, f), F32),
            VMEM((f, f), F32), VMEM((f, f), F32), VMEM((16, f), F32),
        ],
        compiler_params=params(("arbitrary",)),
        cost_estimate=cost(2 * total * f * (4 * f + 2 * slots + 2 * n), 8 * total * f),
    )(me, count, slot_row, recv_row, edges, edge_cot, pre, nodes, agg, halo, w_in, w_out, b_row, gain_row)


def edge_grad_kernel(count_ref, recv_ref, dp_ref, cot_ref, agg_ref, w_ref, out_ref):
    rows, f = dp_ref.shape
    got = dot(one_hot_t(recv_ref[...], agg_ref.shape[0]), agg_ref[...], TN)
    live = lax.broadcasted_iota(jnp.int32, (rows, f), 0) < count_ref[0] - pl.program_id(0) * rows
    mc = jnp.where(live, cot_ref[...].astype(F32) + got, 0.0)
    out_ref[...] = (mc + dot(dp_ref[...], w_ref[...], NT)).astype(BF)


def edge_grad(count, recv_row, dp, edge_cot, agg, w_in, block):
    total, f = dp.shape
    n = agg.shape[0]
    edge_spec = pl.BlockSpec((block, f), lambda i: (i, 0))
    return pl.pallas_call(
        edge_grad_kernel,
        grid=(total // block,),
        in_specs=[
            pl.BlockSpec(memory_space=SMEM),
            pl.BlockSpec((1, block), lambda i: (0, i)),
            edge_spec,
            edge_spec,
            whole((n, f)),
            pl.BlockSpec((f, f), lambda i: (0, 0)),
        ],
        out_specs=edge_spec,
        out_shape=jax.ShapeDtypeStruct((total, f), BF),
        compiler_params=params(("arbitrary",)),
        cost_estimate=cost(2 * total * f * (f + n), 6 * total * f),
    )(count, recv_row, dp, edge_cot, agg, w_in)


def node_grad_kernel(index_ref, returned_ref, sum_r_ref, w_s_ref, w_r_ref, out_ref):
    hot = one_hot_t(index_ref[...], out_ref.shape[0])
    sum_s = dot(hot, returned_ref[...], NN).astype(BF)
    out_ref[...] = dot(sum_s, w_s_ref[...], NT) + dot(sum_r_ref[...], w_r_ref[...], NT)


def node_grad(index_row, returned, sum_r, w_in):
    n, f = sum_r.shape
    slots = returned.shape[0]
    return pl.pallas_call(
        node_grad_kernel,
        grid=(1,),
        in_specs=[
            whole((1, slots)),
            whole((slots, f)),
            whole((n, f)),
            pl.BlockSpec((f, f), lambda i: (1, 0)),
            pl.BlockSpec((f, f), lambda i: (2, 0)),
        ],
        out_specs=whole((n, f)),
        out_shape=jax.ShapeDtypeStruct((n, f), F32),
        compiler_params=params(("arbitrary",)),
        cost_estimate=cost(2 * n * f * (slots + 2 * f), 4 * n * f + 8 * f * f),
    )(index_row, returned, sum_r, w_in, w_in)


def add_split_kernel(extra, keep_ref, got_ref, keep_out, send_out):
    half = keep_out.shape[0] - extra
    total = keep_ref[: extra + half, :] + got_ref[: extra + half, :].astype(F32)
    keep_out[...] = total
    if extra:
        send_out[:extra, :] = total[:extra, :].astype(BF)
    away = keep_ref[extra + half :, :] + got_ref[extra + half :, :].astype(F32)
    send_out[extra:, :] = away.astype(BF)


def add_split(keep, got, extra):
    rows, f = keep.shape
    half = (rows - extra) // 2 + extra
    return pl.pallas_call(
        functools.partial(add_split_kernel, extra),
        out_shape=[jax.ShapeDtypeStruct((half, f), F32), jax.ShapeDtypeStruct((half, f), BF)],
        compiler_params=pltpu.CompilerParams(vmem_limit_bytes=SMALL),
    )(keep, got)


def add_kernel(keep_ref, got_ref, out_ref):
    out_ref[...] = (keep_ref[...].astype(F32) + got_ref[...].astype(F32)).astype(BF)


def add(keep, got):
    return pl.pallas_call(
        add_kernel,
        out_shape=jax.ShapeDtypeStruct(keep.shape, BF),
        compiler_params=pltpu.CompilerParams(vmem_limit_bytes=SMALL),
    )(keep, got)


def swap(x, mask, regions):
    return lax.ppermute(x, "region", [(i, i ^ mask) for i in range(regions)])


def finish_kernel(order_p, order_q, limit, me_ref, p0, p1, q0, q1, vec_ref, w_in_ref, w_out_ref, vec_out):
    f = w_out_ref.shape[1]
    vec = vec_ref[...].astype(F32)
    vec = vec[: EXTRA // 2, :] + vec[EXTRA // 2 :, :]
    squares = jnp.sum(vec * vec, axis=0, keepdims=True)
    for ref in (p0, p1, q0, q1):
        x = ref[...].astype(F32)
        x = x * x
        squares = squares + jnp.sum(jnp.sum(x.reshape(-1, 8, f), axis=0), axis=0, keepdims=True)
    total = jnp.sum(squares, axis=1, keepdims=True)
    scale = jnp.minimum(1.0, limit * lax.rsqrt(total + 1e-06))
    vec_out[...] = (vec[0:3, :] * scale).astype(BF)
    me = me_ref[0]
    targets = [(p0, p1, order_p, ((w_in_ref, f), (w_in_ref, 2 * f))), (q0, q1, order_q, ((w_in_ref, 0), (w_out_ref, 0)))]
    for low, high, order, outs in targets:
        pieces = 2 ** len(order)
        home = me & (pieces - 1)
        r = f // pieces
        for position in range(pieces):
            half, at = divmod(position, pieces // 2)
            piece = home ^ slot_of(position, order)
            for k, (out, offset) in enumerate(outs):
                row = (at * len(outs) + k) * r
                x = (high if half else low)[row : row + r, :].astype(F32)
                start = pl.multiple_of(offset + piece * r, r)
                out[pl.ds(start, r), :] = (x * scale).astype(BF)


def finish(me, p, q, vec, order_p, order_q):
    f = vec.shape[1]
    limit = math.sqrt(4.0 * f * f + 3.0 * f)
    return pl.pallas_call(
        functools.partial(finish_kernel, order_p, order_q, limit),
        in_specs=[pl.BlockSpec(memory_space=SMEM)] + [pl.BlockSpec(memory_space=VMEM)] * 5,
        out_shape=[
            jax.ShapeDtypeStruct((3 * f, f), BF),
            jax.ShapeDtypeStruct((f, f), BF),
            jax.ShapeDtypeStruct((3, f), BF),
        ],
        compiler_params=pltpu.CompilerParams(vmem_limit_bytes=SMALL),
    )(me, *p, *q, vec)


def all_to_all(x, regions):
    rows, f = x.shape
    out = lax.all_to_all(x.reshape(regions, rows // regions, f), "region", split_axis=0, concat_axis=0, tiled=True)
    return out.reshape(rows, f)


def body(nodes, edges, edge_cot, agg_cot, w_in, b_in, w_out, b_out, gain, send_rows, edge_slot, edge_receiver, edge_count):
    regions = lax.axis_size("region")
    f = edges.shape[1]
    me = lax.axis_index("region").astype(jnp.int32).reshape(1)
    masks = [2**k for k in range(regions.bit_length() - 1)]
    last = masks[-1]
    order_p = masks[:-1]
    order_q = order_p[:1] + order_p[1:][::-1]
    index_row = send_rows.reshape(1, -1)
    slot_row = edge_slot.reshape(1, -1)
    recv_row = edge_receiver.reshape(1, -1)
    after = lax.optimization_barrier

    halo = all_to_all(pick_rows(index_row, nodes), regions)
    pre = local_part(recv_row, edges, nodes, w_in, b_in.reshape(1, f), 1024)
    dp, keep_p, send_p, keep_q, send_q, sum_s, sum_r = edge_part(
        me, edge_count, slot_row, recv_row, edges, edge_cot, pre, nodes, agg_cot, halo, w_in, w_out,
        b_out.reshape(1, f), gain.reshape(1, f), order_p, order_q, 512
    )

    steps = len(order_p)
    for step in range(steps):
        got_p = swap(send_p, order_p[step], regions)
        got_q = swap(send_q, order_q[step], regions)
        if step < steps - 1:
            keep_p, send_p = add_split(keep_p, got_p, 0)
            keep_q, send_q = add_split(keep_q, got_q, EXTRA)
        else:
            keep_p, keep_q = add(keep_p, got_p), add(keep_q, got_q)
        if step == 0:
            sum_s, dp, send_p, send_q = after((sum_s, dp, send_p, send_q))
            returned = all_to_all(sum_s, regions)
            grad_edges = edge_grad(edge_count, recv_row, dp, edge_cot, agg_cot, w_in, 512)
        if step == 1:
            keep_p, keep_q, grad_edges = after((keep_p, keep_q, grad_edges))
    part_p = add(keep_p, swap(keep_p, last, regions))
    part_q = add(keep_q, swap(keep_q, last, regions))
    vec, part_q = part_q[:EXTRA], part_q[EXTRA:]
    for step in range(steps - 1, -1, -1):
        got_p = swap(part_p, order_p[step], regions)
        got_q = swap(part_q, order_q[step], regions)
        if step:
            part_p = jnp.concatenate([part_p, got_p], axis=0)
            part_q = jnp.concatenate([part_q, got_q], axis=0)
        if step == steps - 1:
            part_p, part_q, returned = after((part_p, part_q, returned))
            grad_nodes = node_grad(index_row, returned, sum_r, w_in)
        if step == 1:
            part_p, part_q, grad_nodes = after((part_p, part_q, grad_nodes))
    grad_w_in, grad_w_out, grad_vectors = finish(me, (part_p, got_p), (part_q, got_q), vec, order_p, order_q)
    return (grad_edges, grad_nodes, grad_w_in, grad_w_out, grad_vectors)


def solution(mesh):
    split = P(("rep", "region"), None)
    return jax.shard_map(
        body,
        mesh=mesh,
        in_specs=(split, split, split, split, P(), P(), P(), P(), P(), P("region", None), P("region"), P("region"), P("region")),
        out_specs=(split, split, P("rep", None), P("rep", None), P("rep", None)),
        check_vma=False,
    )
```

```python
import functools
import math

import jax
import jax.numpy as jnp
from jax import lax
from jax.experimental import pallas as pl
from jax.experimental.pallas import tpu as pltpu
from jax.sharding import PartitionSpec as P

BF = jnp.bfloat16
F32 = jnp.float32
VMEM = pltpu.VMEM
SMEM = pltpu.SMEM
PICK, LOCAL, EDGE, GRAD, SMALL = 60, 60, 48, 60, 16
PARTS = 2
STRIP = 16
EXTRA = 16


def dot(a, b, dims):
    return lax.dot_general(a, b, ((dims[0], dims[1]), ((), ())), preferred_element_type=F32)


NN = ((1,), (0,))
NT = ((1,), (1,))
TN = ((0,), (0,))


def one_hot_t(index_row, count):
    wide = lax.broadcasted_iota(jnp.int32, (count, index_row.shape[1]), 0) == index_row
    return jnp.where(wide, 1.0, 0.0).astype(BF)


def params(limit):
    return pltpu.CompilerParams(vmem_limit_bytes=limit * 1024 * 1024)


def whole(shape):
    return pl.BlockSpec(shape, lambda *i: (0,) * len(shape))


def cost(flops, nbytes):
    return pl.CostEstimate(flops=int(flops), bytes_accessed=int(nbytes), transcendentals=0)


def flat_row(table):
    a, b = table.shape
    lane = lax.broadcasted_iota(jnp.int32, (b, a * b), 1)
    spread = jnp.where(lane % b == lax.broadcasted_iota(jnp.int32, (b, a * b), 0), 1.0, 0.0).astype(BF)
    wide = dot(table.astype(F32).astype(BF), spread, NN)
    lane = lax.broadcasted_iota(jnp.int32, (a, a * b), 1)
    own = lane // b == lax.broadcasted_iota(jnp.int32, (a, a * b), 0)
    return jnp.sum(jnp.where(own, wide, 0.0), axis=0, keepdims=True).astype(jnp.int32)


def pick_kernel(rows_ref, nodes_ref, out_ref):
    hot = one_hot_t(flat_row(rows_ref[...]), nodes_ref.shape[0])
    out_ref[...] = dot(hot, nodes_ref[...], TN).astype(BF)


def pick_rows(send_rows, nodes):
    return pl.pallas_call(
        pick_kernel,
        out_shape=jax.ShapeDtypeStruct((send_rows.size, nodes.shape[1]), BF),
        compiler_params=params(PICK),
    )(send_rows, nodes)


def fetcher(sems):
    used = []

    def fetch(source, target):
        copy = pltpu.make_async_copy(source, target, sems.at[len(used)])
        used.append(copy)
        copy.start()
        return copy

    return fetch


def strips(first, rows):
    return [pl.ds(first + at, STRIP) for at in range(0, rows, STRIP)]


def local_kernel(count_ref, recv_ref, b_ref, edges_hbm, cot_hbm, nodes_hbm, agg_hbm, w_in_hbm, pre_hbm, mc_hbm,
                 edges, cot, nodes, w_e, w_r, pre, mc, table, got, sems):
    total, f = edges.shape
    n = nodes.shape[0]
    rows = total // PARTS
    fetch = fetcher(sems)
    get_nodes = fetch(nodes_hbm, nodes)
    get_w_r = fetch(w_in_hbm.at[pl.ds(2 * f, f)], w_r)
    get_agg = fetch(agg_hbm, table.at[:, pl.ds(f, f)])
    get_w_e = fetch(w_in_hbm.at[pl.ds(0, f)], w_e)
    gets = []
    for part in range(PARTS):
        at = pl.ds(part * rows, rows)
        gets.append((fetch(edges_hbm.at[at], edges.at[at]), fetch(cot_hbm.at[at], cot.at[at])))
    get_nodes.wait()
    get_w_r.wait()
    table[:, :f] = dot(nodes[...], w_r[...], NN).astype(BF)
    get_agg.wait()
    get_w_e.wait()
    puts = []
    for part in range(PARTS):
        at = pl.ds(part * rows, rows)
        hot = one_hot_t(recv_ref[:, part * rows : (part + 1) * rows], n)
        got[...] = dot(hot, table[...], TN)
        gets[part][0].wait()
        pre[at, :] = (dot(edges[at, :], w_e[...], NN) + got[:, :f] + b_ref[...]).astype(BF)
        puts.append(fetch(pre.at[at], pre_hbm.at[at]))
        gets[part][1].wait()
        live = lax.broadcasted_iota(jnp.int32, (rows, f), 0) < count_ref[0] - part * rows
        mc[at, :] = jnp.where(live, cot[at, :].astype(F32) + got[:, f:], 0.0)
        puts.append(fetch(mc.at[at], mc_hbm.at[at]))
    for put in puts:
        put.wait()


def local_part(count, recv_row, edges, edge_cot, nodes, agg, w_in, b_row):
    total, f = edges.shape
    n = nodes.shape[0]
    anywhere = pl.BlockSpec(memory_space=pl.ANY)
    return pl.pallas_call(
        local_kernel,
        in_specs=[
            pl.BlockSpec(memory_space=SMEM),
            pl.BlockSpec(memory_space=VMEM),
            pl.BlockSpec(memory_space=VMEM),
            anywhere,
            anywhere,
            anywhere,
            anywhere,
            anywhere,
        ],
        out_specs=[anywhere, anywhere],
        out_shape=[jax.ShapeDtypeStruct((total, f), BF), jax.ShapeDtypeStruct((total, f), F32)],
        scratch_shapes=[
            VMEM((total, f), BF), VMEM((total, f), BF), VMEM((n, f), BF), VMEM((f, f), BF), VMEM((f, f), BF),
            VMEM((total, f), BF), VMEM((total, f), F32), VMEM((n, 2 * f), BF), VMEM((total // PARTS, 2 * f), F32),
            pltpu.SemaphoreType.DMA((4 + 4 * PARTS,)),
        ],
        compiler_params=params(LOCAL),
        cost_estimate=cost(2 * total * f * (f + 2 * n), 10 * total * f),
    )(count, recv_row, b_row, edges, edge_cot, nodes, agg, w_in)


def slot_of(position, order):
    slot = 0
    for bit, mask in enumerate(reversed(order)):
        if position >> bit & 1:
            slot |= mask
    return slot


def write_slots(me, parts, keep_ref, send_ref, order, first=0):
    pieces = 2 ** len(order)
    home = me & (pieces - 1)
    r = parts[0].shape[0] // pieces
    for position in range(pieces):
        piece = home ^ slot_of(position, order)
        start = pl.multiple_of(piece * r, r)
        half, at = divmod(position, pieces // 2)
        ref = send_ref if half else keep_ref
        for k, acc in enumerate(parts):
            row = first + (at * len(parts) + k) * r
            ref[row : row + r, :] = acc[pl.ds(start, r), :].astype(ref.dtype)


def edge_kernel(order_p, order_q, me_ref, slot_ref, recv_ref, b_ref, gain_ref, edges_hbm, pre_hbm, mc_hbm, nodes_hbm,
                halo_hbm, w_in_hbm, w_out_hbm, dp_hbm, keep_p, send_p, keep_q, send_q, sum_s_ref, sum_r_ref,
                edges, pre, mc, nodes, halo, w_s, w_out, dp, table, hot, wide, slope, act, dn,
                acc_o, acc_e, acc_n, acc_x, acc_y, sems):
    total, f = edges.shape
    slots, n = halo.shape[0], nodes.shape[0]
    rows = total // PARTS
    inverse = 1.0 / f
    fetch = fetcher(sems)
    get_halo = fetch(halo_hbm, halo)
    get_w_s = fetch(w_in_hbm.at[pl.ds(f, f)], w_s)
    get_pre, get_mc, puts = [], [], []
    for part in range(PARTS):
        at = pl.ds(part * rows, rows)
        get_pre.append(fetch(pre_hbm.at[at], pre.at[at]))
        if part == 0:
            get_w_out = fetch(w_out_hbm, w_out)
        get_mc.append(fetch(mc_hbm.at[at], mc.at[at]))
    get_edges = fetch(edges_hbm, edges)
    get_nodes = fetch(nodes_hbm, nodes)
    sum_dn, sum_mn = [], []

    def gather(part):
        at, columns = pl.ds(part * rows, rows), slice(part * rows, (part + 1) * rows)
        hot[:slots, columns] = one_hot_t(slot_ref[:, columns], slots)
        hot[slots:, columns] = one_hot_t(recv_ref[:, columns], n)
        if part == 0:
            table[...] = dot(halo[...], w_s[...], NN).astype(BF)
        wide[at, :] = dot(hot[:slots, columns], table[...], TN)
        for r in strips(part * rows, rows):
            x = pre[r, :].astype(F32) + wide[r, :]
            sig = 0.5 * jnp.tanh(0.5 * x) + 0.5
            silu = x * sig
            act[r, :] = silu.astype(BF)
            slope[r, :] = sig + silu * (1.0 - sig)

    def norm(part):
        at = pl.ds(part * rows, rows)
        wide[at, :] = dot(act[at, :], w_out[...], NN)
        total_dn = total_mn = jnp.zeros((8, f), F32)
        for r in strips(part * rows, rows):
            x = wide[r, :] + b_ref[...]
            centered = x - jnp.sum(x, axis=1, keepdims=True) * inverse
            inv_std = lax.rsqrt(jnp.sum(centered * centered, axis=1, keepdims=True) * inverse + 1e-05)
            normed = centered * inv_std
            cot = mc[r, :]
            scaled = cot * gain_ref[...]
            mean_s = jnp.sum(scaled, axis=1, keepdims=True) * inverse
            mean_sn = jnp.sum(scaled * normed, axis=1, keepdims=True) * inverse
            d = inv_std * (scaled - mean_s - normed * mean_sn)
            dn[r, :] = d.astype(BF)
            total_dn = total_dn + jnp.sum(d.reshape(STRIP // 8, 8, f), axis=0)
            total_mn = total_mn + jnp.sum((cot * normed).reshape(STRIP // 8, 8, f), axis=0)
        sum_dn.append(total_dn)
        sum_mn.append(total_mn)

    def back(part):
        at = pl.ds(part * rows, rows)
        more = dot(act[at, :], dn[at, :], TN)
        acc_o[...] = more if part == 0 else acc_o[...] + more
        wide[at, :] = dot(dn[at, :], w_out[...], NT)
        for r in strips(part * rows, rows):
            dp[r, :] = (wide[r, :] * slope[r, :]).astype(BF)
        puts.append(fetch(dp.at[at], dp_hbm.at[at]))

    def weights(part):
        at, columns = pl.ds(part * rows, rows), slice(part * rows, (part + 1) * rows)
        more = dot(hot[:, columns], dp[at, :], NN)
        acc_n[...] = more if part == 0 else acc_n[...] + more
        more = dot(edges[at, :], dp[at, :], TN)
        acc_e[...] = more if part == 0 else acc_e[...] + more

    stages = (gather, norm, back, weights)
    for turn in range(PARTS + len(stages) - 1):
        if turn == 0:
            for g in [get_halo, get_w_s] + get_pre:
                g.wait()
        if turn == 1:
            for g in [get_w_out, get_edges, get_nodes] + get_mc:
                g.wait()
        for at in range(len(stages) - 1, -1, -1):
            if 0 <= turn - at < PARTS:
                stages[at](turn - at)

    sum_s = acc_n[:slots, :].astype(BF)
    sum_r = acc_n[slots:, :].astype(BF)
    sum_s_ref[...] = sum_s
    sum_r_ref[...] = sum_r
    acc_x[...] = dot(halo[...], sum_s, TN)
    acc_y[...] = dot(nodes[...], sum_r, TN)
    me = me_ref[0]
    write_slots(me, (acc_x, acc_y), keep_p, send_p, order_p)
    write_slots(me, (acc_e, acc_o), keep_q, send_q, order_q, EXTRA)
    row = lax.broadcasted_iota(jnp.int32, (EXTRA // 2, f), 0)
    exact = jnp.where(row == 0, jnp.sum(acc_n[slots:, :], axis=0, keepdims=True), 0.0)
    exact = jnp.where(row == 1, jnp.sum(sum(sum_dn), axis=0, keepdims=True), exact)
    exact = jnp.where(row == 2, jnp.sum(sum(sum_mn), axis=0, keepdims=True), exact)
    high = exact.astype(BF).astype(F32)
    vectors = jnp.concatenate([high, exact - high], axis=0)
    keep_q[:EXTRA, :] = vectors
    send_q[:EXTRA, :] = vectors.astype(BF)
    for put in puts:
        put.wait()


def edge_part(me, slot_row, recv_row, edges, pre, mc, nodes, halo, w_in, w_out, b_row, gain_row, order_p, order_q):
    total, f = edges.shape
    slots, n = halo.shape[0], nodes.shape[0]
    inside = pl.BlockSpec(memory_space=VMEM)
    anywhere = pl.BlockSpec(memory_space=pl.ANY)
    shapes = [
        ((total, f), BF), ((f, f), F32), ((f, f), BF), ((f + EXTRA, f), F32), ((f + EXTRA, f), BF),
        ((slots, f), BF), ((n, f), BF),
    ]
    return pl.pallas_call(
        functools.partial(edge_kernel, order_p, order_q),
        in_specs=[pl.BlockSpec(memory_space=SMEM)] + [inside] * 4 + [anywhere] * 7,
        out_specs=[anywhere] + [inside] * 6,
        out_shape=[jax.ShapeDtypeStruct(s, d) for s, d in shapes],
        scratch_shapes=[
            VMEM((total, f), BF), VMEM((total, f), BF), VMEM((total, f), F32), VMEM((n, f), BF), VMEM((slots, f), BF),
            VMEM((f, f), BF), VMEM((f, f), BF), VMEM((total, f), BF), VMEM((slots, f), BF),
            VMEM((slots + n, total), BF), VMEM((total, f), F32), VMEM((total, f), F32), VMEM((total, f), BF),
            VMEM((total, f), BF), VMEM((f, f), F32), VMEM((f, f), F32), VMEM((slots + n, f), F32),
            VMEM((f, f), F32), VMEM((f, f), F32), pltpu.SemaphoreType.DMA((5 + 3 * PARTS,)),
        ],
        compiler_params=params(EDGE),
        cost_estimate=cost(2 * total * f * (4 * f + 2 * slots + n), 10 * total * f),
    )(me, slot_row, recv_row, b_row, gain_row, edges, pre, mc, nodes, halo, w_in, w_out)


def edge_grad_kernel(dp_ref, mc_ref, w_ref, out_ref):
    out_ref[...] = (mc_ref[...] + dot(dp_ref[...], w_ref[...], NT)).astype(BF)


def edge_grad(dp, mc, w_in, block):
    total, f = dp.shape
    edge_spec = pl.BlockSpec((block, f), lambda i: (i, 0))
    return pl.pallas_call(
        edge_grad_kernel,
        grid=(total // block,),
        in_specs=[edge_spec, edge_spec, pl.BlockSpec((f, f), lambda i: (0, 0))],
        out_specs=edge_spec,
        out_shape=jax.ShapeDtypeStruct((total, f), BF),
        compiler_params=params(GRAD),
        cost_estimate=cost(2 * total * f * f, 8 * total * f),
    )(dp, mc, w_in)


def node_grad_kernel(rows_ref, returned_ref, sum_r_ref, w_s_ref, w_r_ref, out_ref):
    hot = one_hot_t(flat_row(rows_ref[...]), out_ref.shape[0])
    sum_s = dot(hot, returned_ref[...], NN).astype(BF)
    out_ref[...] = dot(sum_s, w_s_ref[...], NT) + dot(sum_r_ref[...], w_r_ref[...], NT)


def node_grad(send_rows, returned, sum_r, w_in):
    n, f = sum_r.shape
    slots = returned.shape[0]
    return pl.pallas_call(
        node_grad_kernel,
        grid=(1,),
        in_specs=[
            whole(send_rows.shape),
            whole((slots, f)),
            whole((n, f)),
            pl.BlockSpec((f, f), lambda i: (1, 0)),
            pl.BlockSpec((f, f), lambda i: (2, 0)),
        ],
        out_specs=whole((n, f)),
        out_shape=jax.ShapeDtypeStruct((n, f), F32),
        compiler_params=params(GRAD),
        cost_estimate=cost(2 * n * f * (slots + 2 * f), 4 * n * f + 8 * f * f),
    )(send_rows, returned, sum_r, w_in, w_in)


def add_split_kernel(extra, keep_ref, got_ref, keep_out, send_out):
    half = keep_out.shape[0] - extra
    total = keep_ref[: extra + half, :] + got_ref[: extra + half, :].astype(F32)
    keep_out[...] = total
    if extra:
        send_out[:extra, :] = total[:extra, :].astype(BF)
    away = keep_ref[extra + half :, :] + got_ref[extra + half :, :].astype(F32)
    send_out[extra:, :] = away.astype(BF)


def add_split(keep, got, extra):
    rows, f = keep.shape
    half = (rows - extra) // 2 + extra
    return pl.pallas_call(
        functools.partial(add_split_kernel, extra),
        out_shape=[jax.ShapeDtypeStruct((half, f), F32), jax.ShapeDtypeStruct((half, f), BF)],
        compiler_params=params(SMALL),
    )(keep, got)


def add_kernel(keep_ref, got_ref, out_ref):
    out_ref[...] = (keep_ref[...].astype(F32) + got_ref[...].astype(F32)).astype(BF)


def add(keep, got):
    return pl.pallas_call(
        add_kernel,
        out_shape=jax.ShapeDtypeStruct(keep.shape, BF),
        compiler_params=params(SMALL),
    )(keep, got)


def swap(x, mask, regions):
    return lax.ppermute(x, "region", [(i, i ^ mask) for i in range(regions)])


def finish_kernel(order_p, order_q, limit, me_ref, p0, p1, q0, q1, vec_ref, w_in_ref, w_out_ref, vec_out):
    f = w_out_ref.shape[1]
    vec = vec_ref[...].astype(F32)
    vec = vec[: EXTRA // 2, :] + vec[EXTRA // 2 :, :]
    squares = jnp.sum(vec * vec, axis=0, keepdims=True)
    for ref in (p0, p1, q0, q1):
        x = ref[...].astype(F32)
        x = x * x
        squares = squares + jnp.sum(jnp.sum(x.reshape(-1, 8, f), axis=0), axis=0, keepdims=True)
    total = jnp.sum(squares, axis=1, keepdims=True)
    scale = jnp.minimum(1.0, limit * lax.rsqrt(total + 1e-06))
    vec_out[...] = (vec[0:3, :] * scale).astype(BF)
    me = me_ref[0]
    targets = [(p0, p1, order_p, ((w_in_ref, f), (w_in_ref, 2 * f))), (q0, q1, order_q, ((w_in_ref, 0), (w_out_ref, 0)))]
    for low, high, order, outs in targets:
        pieces = 2 ** len(order)
        home = me & (pieces - 1)
        r = f // pieces
        for position in range(pieces):
            half, at = divmod(position, pieces // 2)
            piece = home ^ slot_of(position, order)
            for k, (out, offset) in enumerate(outs):
                row = (at * len(outs) + k) * r
                x = (high if half else low)[row : row + r, :].astype(F32)
                start = pl.multiple_of(offset + piece * r, r)
                out[pl.ds(start, r), :] = (x * scale).astype(BF)


def finish(me, p, q, vec, order_p, order_q):
    f = vec.shape[1]
    limit = math.sqrt(4.0 * f * f + 3.0 * f)
    return pl.pallas_call(
        functools.partial(finish_kernel, order_p, order_q, limit),
        in_specs=[pl.BlockSpec(memory_space=SMEM)] + [pl.BlockSpec(memory_space=VMEM)] * 5,
        out_shape=[
            jax.ShapeDtypeStruct((3 * f, f), BF),
            jax.ShapeDtypeStruct((f, f), BF),
            jax.ShapeDtypeStruct((3, f), BF),
        ],
        compiler_params=params(SMALL),
    )(me, *p, *q, vec)


def all_to_all(x, regions):
    rows, f = x.shape
    out = lax.all_to_all(x.reshape(regions, rows // regions, f), "region", split_axis=0, concat_axis=0, tiled=True)
    return out.reshape(rows, f)


def body(nodes, edges, edge_cot, agg_cot, w_in, b_in, w_out, b_out, gain, send_rows, edge_slot, edge_receiver, edge_count):
    regions = lax.axis_size("region")
    f = edges.shape[1]
    me = lax.axis_index("region").astype(jnp.int32).reshape(1)
    masks = [2**k for k in range(regions.bit_length() - 1)]
    last = masks[-1]
    order_p = masks[:-1]
    order_q = order_p[:1] + order_p[1:][::-1]
    slot_row = edge_slot.reshape(1, -1)
    recv_row = edge_receiver.reshape(1, -1)
    after = lax.optimization_barrier

    halo = all_to_all(pick_rows(send_rows, nodes), regions)
    pre, mc = local_part(edge_count, recv_row, edges, edge_cot, nodes, agg_cot, w_in, b_in.reshape(1, f))
    dp, keep_p, send_p, keep_q, send_q, sum_s, sum_r = edge_part(
        me, slot_row, recv_row, edges, pre, mc, nodes, halo, w_in, w_out,
        b_out.reshape(1, f), gain.reshape(1, f), order_p, order_q
    )

    steps = len(order_p)
    for step in range(steps):
        got_p = swap(send_p, order_p[step], regions)
        got_q = swap(send_q, order_q[step], regions)
        if step == 1:
            got_p, got_q, returned = after((got_p, got_q, returned))
        if step < steps - 1:
            keep_p, send_p = add_split(keep_p, got_p, 0)
            keep_q, send_q = add_split(keep_q, got_q, EXTRA)
        else:
            keep_p, keep_q = add(keep_p, got_p), add(keep_q, got_q)
        if step == 0:
            sum_s, send_p, send_q = after((sum_s, send_p, send_q))
            returned = all_to_all(sum_s, regions)
    got_p = swap(keep_p, last, regions)
    got_q = swap(keep_q, last, regions)
    keep_p, keep_q, dp, sum_r = after((keep_p, keep_q, dp, sum_r))
    grad_edges = edge_grad(dp, mc, w_in, 512)
    grad_nodes = node_grad(send_rows, returned, sum_r, w_in)
    got_p, got_q, grad_edges, grad_nodes = after((got_p, got_q, grad_edges, grad_nodes))
    part_p = add(keep_p, got_p)
    part_q = add(keep_q, got_q)
    vec, part_q = part_q[:EXTRA], part_q[EXTRA:]
    for step in range(steps - 1, -1, -1):
        got_p = swap(part_p, order_p[step], regions)
        got_q = swap(part_q, order_q[step], regions)
        if step:
            part_p = jnp.concatenate([part_p, got_p], axis=0)
            part_q = jnp.concatenate([part_q, got_q], axis=0)
    grad_w_in, grad_w_out, grad_vectors = finish(me, (part_p, got_p), (part_q, got_q), vec, order_p, order_q)
    return (grad_edges, grad_nodes, grad_w_in, grad_w_out, grad_vectors)


def solution(mesh):
    split = P(("rep", "region"), None)
    return jax.shard_map(
        body,
        mesh=mesh,
        in_specs=(split, split, split, split, P(), P(), P(), P(), P(), P("region", None), P("region"), P("region"), P("region")),
        out_specs=(split, split, P("rep", None), P("rep", None), P("rep", None)),
        check_vma=False,
    )
```

```python
import functools
import math

import jax
import jax.numpy as jnp
from jax import lax
from jax.experimental import pallas as pl
from jax.experimental.pallas import tpu as pltpu
from jax.sharding import PartitionSpec as P

BF = jnp.bfloat16
F32 = jnp.float32
VMEM = pltpu.VMEM
SMEM = pltpu.SMEM
PICK, LOCAL, EDGE, GRAD, SMALL = 60, 60, 48, 60, 16
PARTS = 2
STRIP = 16
EXTRA = 16


def dot(a, b, dims):
    return lax.dot_general(a, b, ((dims[0], dims[1]), ((), ())), preferred_element_type=F32)


NN = ((1,), (0,))
NT = ((1,), (1,))
TN = ((0,), (0,))


def one_hot_t(index_row, count):
    wide = lax.broadcasted_iota(jnp.int32, (count, index_row.shape[1]), 0) == index_row
    return jnp.where(wide, 1.0, 0.0).astype(BF)


def params(limit):
    return pltpu.CompilerParams(vmem_limit_bytes=limit * 1024 * 1024)


def whole(shape):
    return pl.BlockSpec(shape, lambda *i: (0,) * len(shape))


def cost(flops, nbytes):
    return pl.CostEstimate(flops=int(flops), bytes_accessed=int(nbytes), transcendentals=0)


def flat_row(table):
    a, b = table.shape
    lane = lax.broadcasted_iota(jnp.int32, (b, a * b), 1)
    spread = jnp.where(lane % b == lax.broadcasted_iota(jnp.int32, (b, a * b), 0), 1.0, 0.0).astype(BF)
    wide = dot(table.astype(F32).astype(BF), spread, NN)
    lane = lax.broadcasted_iota(jnp.int32, (a, a * b), 1)
    own = lane // b == lax.broadcasted_iota(jnp.int32, (a, a * b), 0)
    return jnp.sum(jnp.where(own, wide, 0.0), axis=0, keepdims=True).astype(jnp.int32)


def pick_kernel(rows_ref, nodes_ref, out_ref):
    hot = one_hot_t(flat_row(rows_ref[...]), nodes_ref.shape[0])
    out_ref[...] = dot(hot, nodes_ref[...], TN).astype(BF)


def pick_rows(send_rows, nodes):
    return pl.pallas_call(
        pick_kernel,
        out_shape=jax.ShapeDtypeStruct((send_rows.size, nodes.shape[1]), BF),
        compiler_params=params(PICK),
    )(send_rows, nodes)


def fetcher(sems):
    used = []

    def fetch(source, target):
        copy = pltpu.make_async_copy(source, target, sems.at[len(used)])
        used.append(copy)
        copy.start()
        return copy

    return fetch


def strips(first, rows):
    return [pl.ds(first + at, STRIP) for at in range(0, rows, STRIP)]


def local_kernel(count_ref, recv_ref, b_ref, edges_hbm, cot_hbm, nodes_hbm, agg_hbm, w_in_hbm, pre_hbm, mc_hbm,
                 edges, cot, nodes, w_e, w_r, pre, mc, table, got, sems):
    total, f = edges.shape
    n = nodes.shape[0]
    rows = total // PARTS
    fetch = fetcher(sems)
    get_nodes = fetch(nodes_hbm, nodes)
    get_w_r = fetch(w_in_hbm.at[pl.ds(2 * f, f)], w_r)
    get_agg = fetch(agg_hbm, table.at[:, pl.ds(f, f)])
    get_w_e = fetch(w_in_hbm.at[pl.ds(0, f)], w_e)
    gets = []
    for part in range(PARTS):
        at = pl.ds(part * rows, rows)
        gets.append((fetch(edges_hbm.at[at], edges.at[at]), fetch(cot_hbm.at[at], cot.at[at])))
    get_nodes.wait()
    get_w_r.wait()
    table[:, :f] = dot(nodes[...], w_r[...], NN).astype(BF)
    get_agg.wait()
    get_w_e.wait()
    puts = []
    for part in range(PARTS):
        at = pl.ds(part * rows, rows)
        hot = one_hot_t(recv_ref[:, part * rows : (part + 1) * rows], n)
        got[...] = dot(hot, table[...], TN)
        gets[part][0].wait()
        pre[at, :] = (dot(edges[at, :], w_e[...], NN) + got[:, :f] + b_ref[...]).astype(BF)
        puts.append(fetch(pre.at[at], pre_hbm.at[at]))
        gets[part][1].wait()
        live = lax.broadcasted_iota(jnp.int32, (rows, f), 0) < count_ref[0] - part * rows
        mc[at, :] = jnp.where(live, cot[at, :].astype(F32) + got[:, f:], 0.0)
        puts.append(fetch(mc.at[at], mc_hbm.at[at]))
    for put in puts:
        put.wait()


def local_part(count, recv_row, edges, edge_cot, nodes, agg, w_in, b_row):
    total, f = edges.shape
    n = nodes.shape[0]
    anywhere = pl.BlockSpec(memory_space=pl.ANY)
    return pl.pallas_call(
        local_kernel,
        in_specs=[
            pl.BlockSpec(memory_space=SMEM),
            pl.BlockSpec(memory_space=VMEM),
            pl.BlockSpec(memory_space=VMEM),
            anywhere,
            anywhere,
            anywhere,
            anywhere,
            anywhere,
        ],
        out_specs=[anywhere, anywhere],
        out_shape=[jax.ShapeDtypeStruct((total, f), BF), jax.ShapeDtypeStruct((total, f), F32)],
        scratch_shapes=[
            VMEM((total, f), BF), VMEM((total, f), BF), VMEM((n, f), BF), VMEM((f, f), BF), VMEM((f, f), BF),
            VMEM((total, f), BF), VMEM((total, f), F32), VMEM((n, 2 * f), BF), VMEM((total // PARTS, 2 * f), F32),
            pltpu.SemaphoreType.DMA((4 + 4 * PARTS,)),
        ],
        compiler_params=params(LOCAL),
        cost_estimate=cost(2 * total * f * (f + 2 * n), 10 * total * f),
    )(count, recv_row, b_row, edges, edge_cot, nodes, agg, w_in)


def slot_of(position, order):
    slot = 0
    for bit, mask in enumerate(reversed(order)):
        if position >> bit & 1:
            slot |= mask
    return slot


def write_slots(me, parts, keep_ref, send_ref, order, first=0):
    pieces = 2 ** len(order)
    home = me & (pieces - 1)
    r = parts[0].shape[0] // pieces
    for position in range(pieces):
        piece = home ^ slot_of(position, order)
        start = pl.multiple_of(piece * r, r)
        half, at = divmod(position, pieces // 2)
        ref = send_ref if half else keep_ref
        for k, acc in enumerate(parts):
            row = first + (at * len(parts) + k) * r
            ref[row : row + r, :] = acc[pl.ds(start, r), :].astype(ref.dtype)


def edge_kernel(order_p, order_q, me_ref, slot_ref, recv_ref, b_ref, gain_ref, edges_hbm, pre_hbm, mc_hbm, nodes_hbm,
                halo_hbm, w_in_hbm, w_out_hbm, dp_hbm, keep_p, send_p, keep_q, send_q, sum_s_ref, sum_r_ref,
                edges, pre, mc, nodes, halo, w_s, w_out, dp, table, hot, wide, slope, act, dn,
                acc_o, acc_e, acc_n, acc_x, acc_y, sems):
    total, f = edges.shape
    slots, n = halo.shape[0], nodes.shape[0]
    rows = total // PARTS
    inverse = 1.0 / f
    fetch = fetcher(sems)
    get_halo = fetch(halo_hbm, halo)
    get_w_s = fetch(w_in_hbm.at[pl.ds(f, f)], w_s)
    get_pre, get_mc, puts = [], [], []
    for part in range(PARTS):
        at = pl.ds(part * rows, rows)
        get_pre.append(fetch(pre_hbm.at[at], pre.at[at]))
        if part == 0:
            get_w_out = fetch(w_out_hbm, w_out)
        get_mc.append(fetch(mc_hbm.at[at], mc.at[at]))
    get_edges = fetch(edges_hbm, edges)
    get_nodes = fetch(nodes_hbm, nodes)
    sum_dn, sum_mn = [], []

    def gather(part):
        at, columns = pl.ds(part * rows, rows), slice(part * rows, (part + 1) * rows)
        hot[:slots, columns] = one_hot_t(slot_ref[:, columns], slots)
        hot[slots:, columns] = one_hot_t(recv_ref[:, columns], n)
        if part == 0:
            table[...] = dot(halo[...], w_s[...], NN).astype(BF)
        wide[at, :] = dot(hot[:slots, columns], table[...], TN)
        for r in strips(part * rows, rows):
            x = pre[r, :].astype(F32) + wide[r, :]
            sig = 0.5 * jnp.tanh(0.5 * x) + 0.5
            silu = x * sig
            act[r, :] = silu.astype(BF)
            slope[r, :] = sig + silu * (1.0 - sig)

    def norm(part):
        at = pl.ds(part * rows, rows)
        wide[at, :] = dot(act[at, :], w_out[...], NN)
        total_dn = total_mn = jnp.zeros((8, f), F32)
        for r in strips(part * rows, rows):
            x = wide[r, :] + b_ref[...]
            centered = x - jnp.sum(x, axis=1, keepdims=True) * inverse
            inv_std = lax.rsqrt(jnp.sum(centered * centered, axis=1, keepdims=True) * inverse + 1e-05)
            normed = centered * inv_std
            cot = mc[r, :]
            scaled = cot * gain_ref[...]
            mean_s = jnp.sum(scaled, axis=1, keepdims=True) * inverse
            mean_sn = jnp.sum(scaled * normed, axis=1, keepdims=True) * inverse
            d = inv_std * (scaled - mean_s - normed * mean_sn)
            dn[r, :] = d.astype(BF)
            total_dn = total_dn + jnp.sum(d.reshape(STRIP // 8, 8, f), axis=0)
            total_mn = total_mn + jnp.sum((cot * normed).reshape(STRIP // 8, 8, f), axis=0)
        sum_dn.append(total_dn)
        sum_mn.append(total_mn)

    def back(part):
        at = pl.ds(part * rows, rows)
        more = dot(act[at, :], dn[at, :], TN)
        acc_o[...] = more if part == 0 else acc_o[...] + more
        wide[at, :] = dot(dn[at, :], w_out[...], NT)
        for r in strips(part * rows, rows):
            dp[r, :] = (wide[r, :] * slope[r, :]).astype(BF)
        puts.append(fetch(dp.at[at], dp_hbm.at[at]))

    def weights(part):
        at, columns = pl.ds(part * rows, rows), slice(part * rows, (part + 1) * rows)
        more = dot(hot[:, columns], dp[at, :], NN)
        acc_n[...] = more if part == 0 else acc_n[...] + more
        more = dot(edges[at, :], dp[at, :], TN)
        acc_e[...] = more if part == 0 else acc_e[...] + more

    stages = (gather, norm, back, weights)
    for turn in range(PARTS + len(stages) - 1):
        if turn == 0:
            for g in [get_halo, get_w_s] + get_pre:
                g.wait()
        if turn == 1:
            for g in [get_w_out, get_edges, get_nodes] + get_mc:
                g.wait()
        for at in range(len(stages) - 1, -1, -1):
            if 0 <= turn - at < PARTS:
                stages[at](turn - at)

    sum_s = acc_n[:slots, :].astype(BF)
    sum_r = acc_n[slots:, :].astype(BF)
    sum_s_ref[...] = sum_s
    sum_r_ref[...] = sum_r
    acc_x[...] = dot(halo[...], sum_s, TN)
    acc_y[...] = dot(nodes[...], sum_r, TN)
    me = me_ref[0]
    write_slots(me, (acc_x, acc_y), keep_p, send_p, order_p)
    write_slots(me, (acc_e, acc_o), keep_q, send_q, order_q, EXTRA)
    row = lax.broadcasted_iota(jnp.int32, (EXTRA // 2, f), 0)
    exact = jnp.where(row == 0, jnp.sum(acc_n[slots:, :], axis=0, keepdims=True), 0.0)
    exact = jnp.where(row == 1, jnp.sum(sum(sum_dn), axis=0, keepdims=True), exact)
    exact = jnp.where(row == 2, jnp.sum(sum(sum_mn), axis=0, keepdims=True), exact)
    high = exact.astype(BF).astype(F32)
    vectors = jnp.concatenate([high, exact - high], axis=0)
    keep_q[:EXTRA, :] = vectors
    send_q[:EXTRA, :] = vectors.astype(BF)
    for put in puts:
        put.wait()


def edge_part(me, slot_row, recv_row, edges, pre, mc, nodes, halo, w_in, w_out, b_row, gain_row, order_p, order_q):
    total, f = edges.shape
    slots, n = halo.shape[0], nodes.shape[0]
    inside = pl.BlockSpec(memory_space=VMEM)
    anywhere = pl.BlockSpec(memory_space=pl.ANY)
    shapes = [
        ((total, f), BF), ((f, f), F32), ((f, f), BF), ((f + EXTRA, f), F32), ((f + EXTRA, f), BF),
        ((slots, f), BF), ((n, f), BF),
    ]
    return pl.pallas_call(
        functools.partial(edge_kernel, order_p, order_q),
        in_specs=[pl.BlockSpec(memory_space=SMEM)] + [inside] * 4 + [anywhere] * 7,
        out_specs=[anywhere] + [inside] * 6,
        out_shape=[jax.ShapeDtypeStruct(s, d) for s, d in shapes],
        scratch_shapes=[
            VMEM((total, f), BF), VMEM((total, f), BF), VMEM((total, f), F32), VMEM((n, f), BF), VMEM((slots, f), BF),
            VMEM((f, f), BF), VMEM((f, f), BF), VMEM((total, f), BF), VMEM((slots, f), BF),
            VMEM((slots + n, total), BF), VMEM((total, f), F32), VMEM((total, f), F32), VMEM((total, f), BF),
            VMEM((total, f), BF), VMEM((f, f), F32), VMEM((f, f), F32), VMEM((slots + n, f), F32),
            VMEM((f, f), F32), VMEM((f, f), F32), pltpu.SemaphoreType.DMA((5 + 3 * PARTS,)),
        ],
        compiler_params=params(EDGE),
        cost_estimate=cost(2 * total * f * (4 * f + 2 * slots + n), 10 * total * f),
    )(me, slot_row, recv_row, b_row, gain_row, edges, pre, mc, nodes, halo, w_in, w_out)


def edge_grad_kernel(dp_ref, mc_ref, w_ref, out_ref):
    out_ref[...] = (mc_ref[...] + dot(dp_ref[...], w_ref[...], NT)).astype(BF)


def edge_grad(dp, mc, w_in, block):
    total, f = dp.shape
    edge_spec = pl.BlockSpec((block, f), lambda i: (i, 0))
    return pl.pallas_call(
        edge_grad_kernel,
        grid=(total // block,),
        in_specs=[edge_spec, edge_spec, pl.BlockSpec((f, f), lambda i: (0, 0))],
        out_specs=edge_spec,
        out_shape=jax.ShapeDtypeStruct((total, f), BF),
        compiler_params=params(GRAD),
        cost_estimate=cost(2 * total * f * f, 8 * total * f),
    )(dp, mc, w_in)


def node_grad_kernel(rows_ref, returned_ref, sum_r_ref, w_s_ref, w_r_ref, out_ref):
    hot = one_hot_t(flat_row(rows_ref[...]), out_ref.shape[0])
    sum_s = dot(hot, returned_ref[...], NN).astype(BF)
    out_ref[...] = dot(sum_s, w_s_ref[...], NT) + dot(sum_r_ref[...], w_r_ref[...], NT)


def node_grad(send_rows, returned, sum_r, w_in):
    n, f = sum_r.shape
    slots = returned.shape[0]
    return pl.pallas_call(
        node_grad_kernel,
        grid=(1,),
        in_specs=[
            whole(send_rows.shape),
            whole((slots, f)),
            whole((n, f)),
            pl.BlockSpec((f, f), lambda i: (1, 0)),
            pl.BlockSpec((f, f), lambda i: (2, 0)),
        ],
        out_specs=whole((n, f)),
        out_shape=jax.ShapeDtypeStruct((n, f), F32),
        compiler_params=params(GRAD),
        cost_estimate=cost(2 * n * f * (slots + 2 * f), 4 * n * f + 8 * f * f),
    )(send_rows, returned, sum_r, w_in, w_in)


def add_split_kernel(extra, keep_ref, got_ref, keep_out, send_out):
    half = keep_out.shape[0] - extra
    total = keep_ref[: extra + half, :] + got_ref[: extra + half, :].astype(F32)
    keep_out[...] = total
    if extra:
        send_out[:extra, :] = total[:extra, :].astype(BF)
    away = keep_ref[extra + half :, :] + got_ref[extra + half :, :].astype(F32)
    send_out[extra:, :] = away.astype(BF)


def add_split(keep, got, extra):
    rows, f = keep.shape
    half = (rows - extra) // 2 + extra
    return pl.pallas_call(
        functools.partial(add_split_kernel, extra),
        out_shape=[jax.ShapeDtypeStruct((half, f), F32), jax.ShapeDtypeStruct((half, f), BF)],
        compiler_params=params(SMALL),
    )(keep, got)


def add_kernel(keep_ref, got_ref, out_ref):
    out_ref[...] = (keep_ref[...].astype(F32) + got_ref[...].astype(F32)).astype(BF)


def add(keep, got):
    return pl.pallas_call(
        add_kernel,
        out_shape=jax.ShapeDtypeStruct(keep.shape, BF),
        compiler_params=params(SMALL),
    )(keep, got)


def later_kernel(x_ref, *refs):
    refs[-1][...] = x_ref[...]


def later(x, *others):
    return pl.pallas_call(
        later_kernel,
        in_specs=[pl.BlockSpec(memory_space=VMEM)] + [pl.BlockSpec(memory_space=pl.ANY)] * len(others),
        out_specs=pl.BlockSpec(memory_space=VMEM),
        out_shape=jax.ShapeDtypeStruct(x.shape, x.dtype),
        compiler_params=params(SMALL),
    )(x, *others)


def swap(x, mask, regions):
    return lax.ppermute(x, "region", [(i, i ^ mask) for i in range(regions)])


def finish_kernel(order_p, order_q, limit, me_ref, p0, p1, q0, q1, vec_ref, w_in_ref, w_out_ref, vec_out):
    f = w_out_ref.shape[1]
    vec = vec_ref[...].astype(F32)
    vec = vec[: EXTRA // 2, :] + vec[EXTRA // 2 :, :]
    squares = jnp.sum(vec * vec, axis=0, keepdims=True)
    for ref in (p0, p1, q0, q1):
        x = ref[...].astype(F32)
        x = x * x
        squares = squares + jnp.sum(jnp.sum(x.reshape(-1, 8, f), axis=0), axis=0, keepdims=True)
    total = jnp.sum(squares, axis=1, keepdims=True)
    scale = jnp.minimum(1.0, limit * lax.rsqrt(total + 1e-06))
    vec_out[...] = (vec[0:3, :] * scale).astype(BF)
    me = me_ref[0]
    targets = [(p0, p1, order_p, ((w_in_ref, f), (w_in_ref, 2 * f))), (q0, q1, order_q, ((w_in_ref, 0), (w_out_ref, 0)))]
    for low, high, order, outs in targets:
        pieces = 2 ** len(order)
        home = me & (pieces - 1)
        r = f // pieces
        for position in range(pieces):
            half, at = divmod(position, pieces // 2)
            piece = home ^ slot_of(position, order)
            for k, (out, offset) in enumerate(outs):
                row = (at * len(outs) + k) * r
                x = (high if half else low)[row : row + r, :].astype(F32)
                start = pl.multiple_of(offset + piece * r, r)
                out[pl.ds(start, r), :] = (x * scale).astype(BF)


def finish(me, p, q, vec, order_p, order_q):
    f = vec.shape[1]
    limit = math.sqrt(4.0 * f * f + 3.0 * f)
    return pl.pallas_call(
        functools.partial(finish_kernel, order_p, order_q, limit),
        in_specs=[pl.BlockSpec(memory_space=SMEM)] + [pl.BlockSpec(memory_space=VMEM)] * 5,
        out_shape=[
            jax.ShapeDtypeStruct((3 * f, f), BF),
            jax.ShapeDtypeStruct((f, f), BF),
            jax.ShapeDtypeStruct((3, f), BF),
        ],
        compiler_params=params(SMALL),
    )(me, *p, *q, vec)


def all_to_all(x, regions):
    rows, f = x.shape
    out = lax.all_to_all(x.reshape(regions, rows // regions, f), "region", split_axis=0, concat_axis=0, tiled=True)
    return out.reshape(rows, f)


def body(nodes, edges, edge_cot, agg_cot, w_in, b_in, w_out, b_out, gain, send_rows, edge_slot, edge_receiver, edge_count):
    regions = lax.axis_size("region")
    f = edges.shape[1]
    me = lax.axis_index("region").astype(jnp.int32).reshape(1)
    masks = [2**k for k in range(regions.bit_length() - 1)]
    last = masks[-1]
    order_p = masks[:-1]
    order_q = order_p[:1] + order_p[1:][::-1]
    slot_row = edge_slot.reshape(1, -1)
    recv_row = edge_receiver.reshape(1, -1)
    after = lax.optimization_barrier

    halo = all_to_all(pick_rows(send_rows, nodes), regions)
    pre, mc = local_part(edge_count, recv_row, edges, edge_cot, nodes, agg_cot, w_in, b_in.reshape(1, f))
    dp, keep_p, send_p, keep_q, send_q, sum_s, sum_r = edge_part(
        me, slot_row, recv_row, edges, pre, mc, nodes, halo, w_in, w_out,
        b_out.reshape(1, f), gain.reshape(1, f), order_p, order_q
    )

    steps = len(order_p)
    for step in range(steps):
        got_p = swap(send_p, order_p[step], regions)
        got_q = swap(send_q, order_q[step], regions)
        if step < steps - 1:
            keep_p, send_p = add_split(keep_p, got_p, 0)
            keep_q, send_q = add_split(keep_q, got_q, EXTRA)
        else:
            keep_p, keep_q = add(keep_p, got_p), add(keep_q, got_q)
        if step == 0:
            returned = all_to_all(later(sum_s, send_p, send_q), regions)
    got_p = swap(keep_p, last, regions)
    got_q = swap(keep_q, last, regions)
    keep_p, keep_q, dp, sum_r = after((keep_p, keep_q, dp, sum_r))
    grad_edges = edge_grad(dp, mc, w_in, 512)
    grad_nodes = node_grad(send_rows, returned, sum_r, w_in)
    got_p, got_q, grad_edges, grad_nodes = after((got_p, got_q, grad_edges, grad_nodes))
    part_p = add(keep_p, got_p)
    part_q = add(keep_q, got_q)
    vec, part_q = part_q[:EXTRA], part_q[EXTRA:]
    for step in range(steps - 1, -1, -1):
        got_p = swap(part_p, order_p[step], regions)
        got_q = swap(part_q, order_q[step], regions)
        if step:
            part_p = jnp.concatenate([part_p, got_p], axis=0)
            part_q = jnp.concatenate([part_q, got_q], axis=0)
    grad_w_in, grad_w_out, grad_vectors = finish(me, (part_p, got_p), (part_q, got_q), vec, order_p, order_q)
    return (grad_edges, grad_nodes, grad_w_in, grad_w_out, grad_vectors)


def solution(mesh):
    split = P(("rep", "region"), None)
    return jax.shard_map(
        body,
        mesh=mesh,
        in_specs=(split, split, split, split, P(), P(), P(), P(), P(), P("region", None), P("region"), P("region"), P("region")),
        out_specs=(split, split, P("rep", None), P("rep", None), P("rep", None)),
        check_vma=False,
    )
```

```python
import functools
import math

import jax
import jax.numpy as jnp
from jax import lax
from jax.experimental import pallas as pl
from jax.experimental.pallas import tpu as pltpu
from jax.sharding import PartitionSpec as P

BF = jnp.bfloat16
F32 = jnp.float32
VMEM = pltpu.VMEM
SMEM = pltpu.SMEM
PICK, LOCAL, EDGE, GRAD, SMALL = 60, 60, 48, 60, 16
PARTS = 2
STRIP = 16
EXTRA = 16


def dot(a, b, dims):
    return lax.dot_general(a, b, ((dims[0], dims[1]), ((), ())), preferred_element_type=F32)


NN = ((1,), (0,))
NT = ((1,), (1,))
TN = ((0,), (0,))


def one_hot_t(index_row, count):
    wide = lax.broadcasted_iota(jnp.int32, (count, index_row.shape[1]), 0) == index_row
    return jnp.where(wide, 1.0, 0.0).astype(BF)


def params(limit):
    return pltpu.CompilerParams(vmem_limit_bytes=limit * 1024 * 1024)


def whole(shape):
    return pl.BlockSpec(shape, lambda *i: (0,) * len(shape))


def cost(flops, nbytes):
    return pl.CostEstimate(flops=int(flops), bytes_accessed=int(nbytes), transcendentals=0)


def flat_row(table):
    a, b = table.shape
    lane = lax.broadcasted_iota(jnp.int32, (b, a * b), 1)
    spread = jnp.where(lane % b == lax.broadcasted_iota(jnp.int32, (b, a * b), 0), 1.0, 0.0).astype(BF)
    wide = dot(table.astype(F32).astype(BF), spread, NN)
    lane = lax.broadcasted_iota(jnp.int32, (a, a * b), 1)
    own = lane // b == lax.broadcasted_iota(jnp.int32, (a, a * b), 0)
    return jnp.sum(jnp.where(own, wide, 0.0), axis=0, keepdims=True).astype(jnp.int32)


def pick_kernel(rows_ref, nodes_ref, out_ref):
    hot = one_hot_t(flat_row(rows_ref[...]), nodes_ref.shape[0])
    out_ref[...] = dot(hot, nodes_ref[...], TN).astype(BF)


def pick_rows(send_rows, nodes):
    return pl.pallas_call(
        pick_kernel,
        out_shape=jax.ShapeDtypeStruct((send_rows.size, nodes.shape[1]), BF),
        compiler_params=params(PICK),
    )(send_rows, nodes)


def fetcher(sems):
    used = []

    def fetch(source, target):
        copy = pltpu.make_async_copy(source, target, sems.at[len(used)])
        used.append(copy)
        copy.start()
        return copy

    return fetch


def strips(first, rows):
    return [pl.ds(first + at, STRIP) for at in range(0, rows, STRIP)]


def local_kernel(count_ref, recv_ref, b_ref, edges_hbm, cot_hbm, nodes_hbm, agg_hbm, w_in_hbm, pre_hbm, mc_hbm,
                 edges, cot, nodes, w_e, w_r, pre, mc, table, got, sems):
    total, f = edges.shape
    n = nodes.shape[0]
    rows = total // PARTS
    fetch = fetcher(sems)
    get_nodes = fetch(nodes_hbm, nodes)
    get_w_r = fetch(w_in_hbm.at[pl.ds(2 * f, f)], w_r)
    get_agg = fetch(agg_hbm, table.at[:, pl.ds(f, f)])
    get_w_e = fetch(w_in_hbm.at[pl.ds(0, f)], w_e)
    gets = []
    for part in range(PARTS):
        at = pl.ds(part * rows, rows)
        gets.append((fetch(edges_hbm.at[at], edges.at[at]), fetch(cot_hbm.at[at], cot.at[at])))
    get_nodes.wait()
    get_w_r.wait()
    table[:, :f] = dot(nodes[...], w_r[...], NN).astype(BF)
    get_agg.wait()
    get_w_e.wait()
    puts = []
    for part in range(PARTS):
        at = pl.ds(part * rows, rows)
        hot = one_hot_t(recv_ref[:, part * rows : (part + 1) * rows], n)
        got[...] = dot(hot, table[...], TN)
        gets[part][0].wait()
        pre[at, :] = (dot(edges[at, :], w_e[...], NN) + got[:, :f] + b_ref[...]).astype(BF)
        puts.append(fetch(pre.at[at], pre_hbm.at[at]))
        gets[part][1].wait()
        live = lax.broadcasted_iota(jnp.int32, (rows, f), 0) < count_ref[0] - part * rows
        mc[at, :] = jnp.where(live, cot[at, :].astype(F32) + got[:, f:], 0.0)
        puts.append(fetch(mc.at[at], mc_hbm.at[at]))
    for put in puts:
        put.wait()


def local_part(count, recv_row, edges, edge_cot, nodes, agg, w_in, b_row):
    total, f = edges.shape
    n = nodes.shape[0]
    anywhere = pl.BlockSpec(memory_space=pl.ANY)
    return pl.pallas_call(
        local_kernel,
        in_specs=[
            pl.BlockSpec(memory_space=SMEM),
            pl.BlockSpec(memory_space=VMEM),
            pl.BlockSpec(memory_space=VMEM),
            anywhere,
            anywhere,
            anywhere,
            anywhere,
            anywhere,
        ],
        out_specs=[anywhere, anywhere],
        out_shape=[jax.ShapeDtypeStruct((total, f), BF), jax.ShapeDtypeStruct((total, f), F32)],
        scratch_shapes=[
            VMEM((total, f), BF), VMEM((total, f), BF), VMEM((n, f), BF), VMEM((f, f), BF), VMEM((f, f), BF),
            VMEM((total, f), BF), VMEM((total, f), F32), VMEM((n, 2 * f), BF), VMEM((total // PARTS, 2 * f), F32),
            pltpu.SemaphoreType.DMA((4 + 4 * PARTS,)),
        ],
        compiler_params=params(LOCAL),
        cost_estimate=cost(2 * total * f * (f + 2 * n), 10 * total * f),
    )(count, recv_row, b_row, edges, edge_cot, nodes, agg, w_in)


def slot_of(position, order):
    slot = 0
    for bit, mask in enumerate(reversed(order)):
        if position >> bit & 1:
            slot |= 1 << sorted(order).index(mask)
    return slot


def home_of(me, order):
    return sum(((me // mask) & 1) << bit for bit, mask in enumerate(sorted(order)))


def write_slots(me, parts, keep_ref, send_ref, order, first=0):
    pieces = 2 ** len(order)
    home = home_of(me, order)
    r = parts[0].shape[0] // pieces
    for position in range(pieces):
        piece = home ^ slot_of(position, order)
        start = pl.multiple_of(piece * r, r)
        half, at = divmod(position, pieces // 2)
        ref = send_ref if half else keep_ref
        for k, acc in enumerate(parts):
            row = first + (at * len(parts) + k) * r
            ref[row : row + r, :] = acc[pl.ds(start, r), :].astype(ref.dtype)


def edge_kernel(order_p, order_q, me_ref, slot_ref, recv_ref, b_ref, gain_ref, edges_hbm, pre_hbm, mc_hbm, nodes_hbm,
                halo_hbm, w_in_hbm, w_out_hbm, dp_hbm, keep_p, send_p, keep_q, send_q, sum_s_ref, sum_r_ref,
                edges, pre, mc, nodes, halo, w_s, w_out, dp, table, hot, wide, slope, act, dn,
                acc_o, acc_e, acc_n, acc_x, acc_y, sems):
    total, f = edges.shape
    slots, n = halo.shape[0], nodes.shape[0]
    rows = total // PARTS
    inverse = 1.0 / f
    fetch = fetcher(sems)
    get_halo = fetch(halo_hbm, halo)
    get_w_s = fetch(w_in_hbm.at[pl.ds(f, f)], w_s)
    get_pre, get_mc, puts = [], [], []
    for part in range(PARTS):
        at = pl.ds(part * rows, rows)
        get_pre.append(fetch(pre_hbm.at[at], pre.at[at]))
        if part == 0:
            get_w_out = fetch(w_out_hbm, w_out)
        get_mc.append(fetch(mc_hbm.at[at], mc.at[at]))
    get_edges = fetch(edges_hbm, edges)
    get_nodes = fetch(nodes_hbm, nodes)
    sum_dn, sum_mn = [], []

    def gather(part):
        at, columns = pl.ds(part * rows, rows), slice(part * rows, (part + 1) * rows)
        if part == 0:
            table[...] = dot(halo[...], w_s[...], NN).astype(BF)
        wide[at, :] = dot(hot[:slots, columns], table[...], TN)
        for r in strips(part * rows, rows):
            x = pre[r, :].astype(F32) + wide[r, :]
            sig = 0.5 * jnp.tanh(0.5 * x) + 0.5
            silu = x * sig
            act[r, :] = silu.astype(BF)
            slope[r, :] = sig + silu * (1.0 - sig)

    def norm(part):
        at = pl.ds(part * rows, rows)
        wide[at, :] = dot(act[at, :], w_out[...], NN)
        total_dn = total_mn = jnp.zeros((8, f), F32)
        for r in strips(part * rows, rows):
            x = wide[r, :] + b_ref[...]
            centered = x - jnp.sum(x, axis=1, keepdims=True) * inverse
            inv_std = lax.rsqrt(jnp.sum(centered * centered, axis=1, keepdims=True) * inverse + 1e-05)
            normed = centered * inv_std
            cot = mc[r, :]
            scaled = cot * gain_ref[...]
            mean_s = jnp.sum(scaled, axis=1, keepdims=True) * inverse
            mean_sn = jnp.sum(scaled * normed, axis=1, keepdims=True) * inverse
            d = inv_std * (scaled - mean_s - normed * mean_sn)
            dn[r, :] = d.astype(BF)
            total_dn = total_dn + jnp.sum(d.reshape(STRIP // 8, 8, f), axis=0)
            total_mn = total_mn + jnp.sum((cot * normed).reshape(STRIP // 8, 8, f), axis=0)
        sum_dn.append(total_dn)
        sum_mn.append(total_mn)

    def back(part):
        at = pl.ds(part * rows, rows)
        more = dot(act[at, :], dn[at, :], TN)
        acc_o[...] = more if part == 0 else acc_o[...] + more
        wide[at, :] = dot(dn[at, :], w_out[...], NT)
        for r in strips(part * rows, rows):
            dp[r, :] = (wide[r, :] * slope[r, :]).astype(BF)
        puts.append(fetch(dp.at[at], dp_hbm.at[at]))

    def weights(part):
        at, columns = pl.ds(part * rows, rows), slice(part * rows, (part + 1) * rows)
        more = dot(hot[:, columns], dp[at, :], NN)
        acc_n[...] = more if part == 0 else acc_n[...] + more
        more = dot(edges[at, :], dp[at, :], TN)
        acc_e[...] = more if part == 0 else acc_e[...] + more

    for part in range(PARTS):
        columns = slice(part * rows, (part + 1) * rows)
        hot[:slots, columns] = one_hot_t(slot_ref[:, columns], slots)
        hot[slots:, columns] = one_hot_t(recv_ref[:, columns], n)
    stages = (gather, norm, back, weights)
    for turn in range(PARTS + len(stages) - 1):
        if turn == 0:
            for g in [get_halo, get_w_s, get_pre[0]]:
                g.wait()
        if turn == 1:
            for g in [get_w_out] + get_pre[1:] + get_mc[:1]:
                g.wait()
        if turn == 2:
            for g in get_mc[1:] + [get_edges, get_nodes]:
                g.wait()
        for at in range(len(stages) - 1, -1, -1):
            if 0 <= turn - at < PARTS:
                stages[at](turn - at)

    sum_s = acc_n[:slots, :].astype(BF)
    sum_r = acc_n[slots:, :].astype(BF)
    sum_s_ref[...] = sum_s
    sum_r_ref[...] = sum_r
    acc_x[...] = dot(halo[...], sum_s, TN)
    acc_y[...] = dot(nodes[...], sum_r, TN)
    me = me_ref[0]
    write_slots(me, (acc_x, acc_y), keep_p, send_p, order_p)
    write_slots(me, (acc_e, acc_o), keep_q, send_q, order_q, EXTRA)
    row = lax.broadcasted_iota(jnp.int32, (EXTRA // 2, f), 0)
    exact = jnp.where(row == 0, jnp.sum(acc_n[slots:, :], axis=0, keepdims=True), 0.0)
    exact = jnp.where(row == 1, jnp.sum(sum(sum_dn), axis=0, keepdims=True), exact)
    exact = jnp.where(row == 2, jnp.sum(sum(sum_mn), axis=0, keepdims=True), exact)
    high = exact.astype(BF).astype(F32)
    vectors = jnp.concatenate([high, exact - high], axis=0)
    keep_q[:EXTRA, :] = vectors
    send_q[:EXTRA, :] = vectors.astype(BF)
    for put in puts:
        put.wait()


def edge_part(me, slot_row, recv_row, edges, pre, mc, nodes, halo, w_in, w_out, b_row, gain_row, order_p, order_q):
    total, f = edges.shape
    slots, n = halo.shape[0], nodes.shape[0]
    inside = pl.BlockSpec(memory_space=VMEM)
    anywhere = pl.BlockSpec(memory_space=pl.ANY)
    shapes = [
        ((total, f), BF), ((f, f), F32), ((f, f), BF), ((f + EXTRA, f), F32), ((f + EXTRA, f), BF),
        ((slots, f), BF), ((n, f), BF),
    ]
    return pl.pallas_call(
        functools.partial(edge_kernel, order_p, order_q),
        in_specs=[pl.BlockSpec(memory_space=SMEM)] + [inside] * 4 + [anywhere] * 7,
        out_specs=[anywhere] + [inside] * 6,
        out_shape=[jax.ShapeDtypeStruct(s, d) for s, d in shapes],
        scratch_shapes=[
            VMEM((total, f), BF), VMEM((total, f), BF), VMEM((total, f), F32), VMEM((n, f), BF), VMEM((slots, f), BF),
            VMEM((f, f), BF), VMEM((f, f), BF), VMEM((total, f), BF), VMEM((slots, f), BF),
            VMEM((slots + n, total), BF), VMEM((total, f), F32), VMEM((total, f), F32), VMEM((total, f), BF),
            VMEM((total, f), BF), VMEM((f, f), F32), VMEM((f, f), F32), VMEM((slots + n, f), F32),
            VMEM((f, f), F32), VMEM((f, f), F32), pltpu.SemaphoreType.DMA((5 + 3 * PARTS,)),
        ],
        compiler_params=params(EDGE),
        cost_estimate=cost(2 * total * f * (4 * f + 2 * slots + n), 10 * total * f),
    )(me, slot_row, recv_row, b_row, gain_row, edges, pre, mc, nodes, halo, w_in, w_out)


def edge_grad_kernel(dp_ref, mc_ref, w_ref, out_ref):
    out_ref[...] = (mc_ref[...] + dot(dp_ref[...], w_ref[...], NT)).astype(BF)


def edge_grad(dp, mc, w_in, block):
    total, f = dp.shape
    edge_spec = pl.BlockSpec((block, f), lambda i: (i, 0))
    return pl.pallas_call(
        edge_grad_kernel,
        grid=(total // block,),
        in_specs=[edge_spec, edge_spec, pl.BlockSpec((f, f), lambda i: (0, 0))],
        out_specs=edge_spec,
        out_shape=jax.ShapeDtypeStruct((total, f), BF),
        compiler_params=params(GRAD),
        cost_estimate=cost(2 * total * f * f, 8 * total * f),
    )(dp, mc, w_in)


def node_grad_kernel(rows_ref, returned_ref, sum_r_ref, w_s_ref, w_r_ref, out_ref):
    hot = one_hot_t(flat_row(rows_ref[...]), out_ref.shape[0])
    sum_s = dot(hot, returned_ref[...], NN).astype(BF)
    out_ref[...] = dot(sum_s, w_s_ref[...], NT) + dot(sum_r_ref[...], w_r_ref[...], NT)


def node_grad(send_rows, returned, sum_r, w_in):
    n, f = sum_r.shape
    slots = returned.shape[0]
    return pl.pallas_call(
        node_grad_kernel,
        grid=(1,),
        in_specs=[
            whole(send_rows.shape),
            whole((slots, f)),
            whole((n, f)),
            pl.BlockSpec((f, f), lambda i: (1, 0)),
            pl.BlockSpec((f, f), lambda i: (2, 0)),
        ],
        out_specs=whole((n, f)),
        out_shape=jax.ShapeDtypeStruct((n, f), F32),
        compiler_params=params(GRAD),
        cost_estimate=cost(2 * n * f * (slots + 2 * f), 4 * n * f + 8 * f * f),
    )(send_rows, returned, sum_r, w_in, w_in)


def add_split_kernel(extra, keep_ref, got_ref, keep_out, send_out):
    half = keep_out.shape[0] - extra
    total = keep_ref[: extra + half, :] + got_ref[: extra + half, :].astype(F32)
    keep_out[...] = total
    if extra:
        send_out[:extra, :] = total[:extra, :].astype(BF)
    away = keep_ref[extra + half :, :] + got_ref[extra + half :, :].astype(F32)
    send_out[extra:, :] = away.astype(BF)


def add_split(keep, got, extra):
    rows, f = keep.shape
    half = (rows - extra) // 2 + extra
    return pl.pallas_call(
        functools.partial(add_split_kernel, extra),
        out_shape=[jax.ShapeDtypeStruct((half, f), F32), jax.ShapeDtypeStruct((half, f), BF)],
        compiler_params=params(SMALL),
    )(keep, got)


def add_kernel(keep_ref, got_ref, out_ref):
    out_ref[...] = (keep_ref[...].astype(F32) + got_ref[...].astype(F32)).astype(BF)


def add(keep, got):
    return pl.pallas_call(
        add_kernel,
        out_shape=jax.ShapeDtypeStruct(keep.shape, BF),
        compiler_params=params(SMALL),
    )(keep, got)


def later_kernel(x_ref, *refs):
    refs[-1][...] = x_ref[...]


def later(x, *others):
    return pl.pallas_call(
        later_kernel,
        in_specs=[pl.BlockSpec(memory_space=VMEM)] + [pl.BlockSpec(memory_space=pl.ANY)] * len(others),
        out_specs=pl.BlockSpec(memory_space=VMEM),
        out_shape=jax.ShapeDtypeStruct(x.shape, x.dtype),
        compiler_params=params(SMALL),
    )(x, *others)


def swap(x, mask, regions):
    return lax.ppermute(x, "region", [(i, i ^ mask) for i in range(regions)])


def square_sums(refs):
    total = jnp.zeros((8, refs[0].shape[1]), F32)
    for ref in refs:
        for at in range(0, ref.shape[0], STRIP):
            x = ref[at : at + STRIP, :].astype(F32)
            total = total + jnp.sum((x * x).reshape(STRIP // 8, 8, -1), axis=0)
    return total


def squares_kernel(*refs):
    refs[-1][...] = square_sums(refs[:-1])


def squares(*arrays):
    return pl.pallas_call(
        squares_kernel,
        out_shape=jax.ShapeDtypeStruct((8, arrays[0].shape[1]), F32),
        compiler_params=params(SMALL),
    )(*arrays)


def finish_kernel(order_p, order_q, limit, me_ref, p0, p1, p2, p3, q0, q1, q2, q3, vec_ref, known_ref, w_in_ref,
                  w_out_ref, vec_out):
    f = w_out_ref.shape[1]
    vec = vec_ref[...].astype(F32)
    vec = vec[: EXTRA // 2, :] + vec[EXTRA // 2 :, :]
    total = known_ref[...] + square_sums((p3, q3)) + vec * vec
    total = jnp.sum(jnp.sum(total, axis=0, keepdims=True), axis=1, keepdims=True)
    scale = jnp.minimum(1.0, limit * lax.rsqrt(total + 1e-06))
    vec_out[...] = (vec[0:3, :] * scale).astype(BF)
    me = me_ref[0]
    targets = [
        ((p0, p1, p2, p3), order_p, ((w_in_ref, f), (w_in_ref, 2 * f))),
        ((q0, q1, q2, q3), order_q, ((w_in_ref, 0), (w_out_ref, 0))),
    ]
    for refs, order, outs in targets:
        pieces = 2 ** len(order)
        home = home_of(me, order)
        r = f // pieces
        for position in range(pieces):
            ref, at = divmod(position, pieces // 4)
            piece = home ^ slot_of(position, order)
            for k, (out, offset) in enumerate(outs):
                row = (at * len(outs) + k) * r
                x = refs[ref][row : row + r, :].astype(F32)
                start = pl.multiple_of(offset + piece * r, r)
                out[pl.ds(start, r), :] = (x * scale).astype(BF)


def finish(me, p, q, vec, known, order_p, order_q):
    f = vec.shape[1]
    limit = math.sqrt(4.0 * f * f + 3.0 * f)
    return pl.pallas_call(
        functools.partial(finish_kernel, order_p, order_q, limit),
        in_specs=[pl.BlockSpec(memory_space=SMEM)] + [pl.BlockSpec(memory_space=VMEM)] * 10,
        out_shape=[
            jax.ShapeDtypeStruct((3 * f, f), BF),
            jax.ShapeDtypeStruct((f, f), BF),
            jax.ShapeDtypeStruct((3, f), BF),
        ],
        compiler_params=params(SMALL),
    )(me, *p, *q, vec, known)


def all_to_all(x, regions):
    rows, f = x.shape
    out = lax.all_to_all(x.reshape(regions, rows // regions, f), "region", split_axis=0, concat_axis=0, tiled=True)
    return out.reshape(rows, f)


def body(nodes, edges, edge_cot, agg_cot, w_in, b_in, w_out, b_out, gain, send_rows, edge_slot, edge_receiver, edge_count):
    regions = lax.axis_size("region")
    f = edges.shape[1]
    me = lax.axis_index("region").astype(jnp.int32).reshape(1)
    masks = [2**k for k in range(regions.bit_length() - 1)]
    order_p, last_p = masks[:-1], masks[-1]
    order_q, last_q = order_p[:1] + order_p[1:][::-1], last_p
    slot_row = edge_slot.reshape(1, -1)
    recv_row = edge_receiver.reshape(1, -1)
    after = lax.optimization_barrier

    halo = all_to_all(pick_rows(send_rows, nodes), regions)
    pre, mc = local_part(edge_count, recv_row, edges, edge_cot, nodes, agg_cot, w_in, b_in.reshape(1, f))
    dp, keep_p, send_p, keep_q, send_q, sum_s, sum_r = edge_part(
        me, slot_row, recv_row, edges, pre, mc, nodes, halo, w_in, w_out,
        b_out.reshape(1, f), gain.reshape(1, f), order_p, order_q
    )

    steps = len(order_p)
    for step in range(steps):
        got_p = swap(send_p, order_p[step], regions)
        got_q = swap(send_q, order_q[step], regions)
        if step < steps - 1:
            keep_p, send_p = add_split(keep_p, got_p, 0)
            keep_q, send_q = add_split(keep_q, got_q, EXTRA)
        else:
            keep_p, keep_q = add(keep_p, got_p), add(keep_q, got_q)
        if step == 0:
            returned = all_to_all(later(sum_s, send_p, send_q), regions)
    got_p = swap(keep_p, last_p, regions)
    got_q = swap(keep_q, last_q, regions)
    keep_p, keep_q, dp, sum_r = after((keep_p, keep_q, dp, sum_r))
    grad_edges = edge_grad(dp, mc, w_in, 512)
    grad_nodes = node_grad(send_rows, returned, sum_r, w_in)
    got_p, got_q, grad_edges, grad_nodes = after((got_p, got_q, grad_edges, grad_nodes))
    part_p = add(keep_p, got_p)
    part_q = add(keep_q, got_q)
    vec, part_q = part_q[:EXTRA], part_q[EXTRA:]
    for step in range(steps - 1, 1, -1):
        part_p = jnp.concatenate([part_p, swap(part_p, order_p[step], regions)], axis=0)
        part_q = jnp.concatenate([part_q, swap(part_q, order_q[step], regions)], axis=0)
    got_p = swap(part_p, order_p[1], regions)
    got_q = swap(part_q, order_q[1], regions)
    near_p = swap(part_p, order_p[0], regions)
    near_q = swap(part_q, order_q[0], regions)
    all_p = (part_p, got_p, near_p, swap(got_p, order_p[0], regions))
    all_q = (part_q, got_q, near_q, swap(got_q, order_q[0], regions))
    known = squares(*all_p[:3], *all_q[:3])
    grad_w_in, grad_w_out, grad_vectors = finish(me, all_p, all_q, vec, known, order_p, order_q)
    return (grad_edges, grad_nodes, grad_w_in, grad_w_out, grad_vectors)


def solution(mesh):
    split = P(("rep", "region"), None)
    return jax.shard_map(
        body,
        mesh=mesh,
        in_specs=(split, split, split, split, P(), P(), P(), P(), P(), P("region", None), P("region"), P("region"), P("region")),
        out_specs=(split, split, P("rep", None), P("rep", None), P("rep", None)),
        check_vma=False,
    )
```
